256 devices in a mesh: elem: 32 (over y_lo, z, core), state: 8 (over y_hi, x).
Axes of the slice: x: 4, y: 4 (y_hi: 2, y_lo: 2; y = y_hi * 2 + y_lo), z: 8, core: 2. Of those that a mesh axis runs over, the one named last changes fastest.
Arguments:
- coefficients: bfloat16 [2048, 64, 1024], P('elem', None, 'state'), may hold values from -1200 to 1200
- hamiltonian: bfloat16 [2048, 64, 448], P('elem'), may hold values from -0.25 to 0.25
- neighbours: int32 [2048, 6], P('elem'), may hold values from 0 to 2047, as said below
- pattern: int32 [2048, 6], P('elem'), may hold values 0 or 1
Outputs:
- orthonormal: bfloat16 [2048, 64, 1024], P('elem', None, 'state')
The draws below stay inside these ranges and needn't reach their ends.
Inputs may be any that keep to these rules, and one draw needn't show every extreme that they name: Elements form layers of 32 consecutive ids, cyclically ordered; across face 0 lie the elements of the next layer, across face 1 those of the previous layer, across faces 2 to 5 those of the same layer; for each face, the neighbours of one layer's elements are all elements of the target layer, each once.
All inputs are finite; a program needn't handle non-finite values. No bound on the sum of `pattern` on one device may be relied on, other than what follows from the above.
Results may differ from the reference program's by a relative error of at most 0.0061.
Values may be sent and summed in bfloat16 or wider, within the bound.
A program may use at most 128 MiB of HBM per device.

```python
import jax
import jax.numpy as jnp
from jax import lax

NB = 64
NS = 1024
LAYER = 32
E = 2048


def draw_coefficients(key, part):
    key = jax.random.fold_in(key, 11)
    key_base, key_rows, key_cols = jax.random.split(key, 3)
    position = jnp.arange(E, dtype=jnp.float32) / (E - 1)
    row_draw = jax.random.uniform(key_rows, (E,), jnp.float32)
    col_draw = jax.random.uniform(key_cols, (NS,), jnp.float32)
    base = jnp.clip(jax.random.normal(key_base, (E, NB, NS), jnp.float32), -4.0, 4.0)
    row_scale = jnp.power(10.0, row_draw) * jnp.power(3.0, position)
    col_scale = jnp.power(10.0, col_draw)
    values = base * row_scale[:, None, None] * col_scale[None, None, :]
    return values.astype(jnp.bfloat16)


def draw_neighbours(key, part):
    key = jax.random.fold_in(key, 5)
    layers = E // LAYER
    keys = jax.random.split(key, layers * 6)
    perms = jax.vmap(lambda single: jax.random.permutation(single, LAYER))(keys)
    perms = perms.reshape(layers, 6, LAYER).astype(jnp.int32)
    layer_ids = jnp.arange(layers, dtype=jnp.int32)
    steps_by_face = jnp.array([1, -1, 0, 0, 0, 0], dtype=jnp.int32)
    targets = jnp.mod(layer_ids[:, None] + steps_by_face[None, :], layers)
    ids = targets[:, :, None] * LAYER + perms
    return jnp.transpose(ids, (0, 2, 1)).reshape(E, 6)


def with_ends(values, rng, smallest, high):
    extent = values.shape
    place = [jax.random.randint(jax.random.fold_in(rng, axis), (), 0, extent[axis]) for axis in range(len(extent))]
    values = values.at[tuple(place)].set(smallest)
    longest = extent.index(max(extent))
    place[longest] = (place[longest] + 1) % extent[longest]
    return values.at[tuple(place)].set(high)


def block_levels(stream_key, extent, cuts, least, largest):
    loudness = 1.0
    for axis_at, blocks in cuts:
        steps = jax.random.uniform(jax.random.fold_in(jax.random.fold_in(stream_key, 6), axis_at), (blocks,), jnp.float32, least / len(cuts), largest / len(cuts))
        loudness = loudness * jnp.repeat(jnp.exp(steps), extent[axis_at] // blocks).reshape((-1,) + (1,) * (len(extent) - 1 - axis_at))
    return loudness


def normal_values(rng, shape, width, bound, cuts=(), held_as=jnp.bfloat16):
    factor_of = block_levels(rng, shape, cuts, -0.22, 0.18) if cuts else 1.0
    drawn = jax.random.normal(rng, shape, jnp.float32) * width * factor_of
    return jnp.minimum(jnp.maximum(drawn, -bound), bound).astype(held_as)


def setup_inputs(seed: int = 0) -> dict:
    key_list = jax.random.split(jax.random.key(seed), 5)
    return {
        "coefficients": draw_coefficients(jax.random.fold_in(key_list[4], 71), 0),
        "hamiltonian": normal_values(key_list[1], (E, NB, 7 * NB), (7 * NB) ** -0.5, 0.25, ((0, 32),)),
        "neighbours": draw_neighbours(jax.random.fold_in(key_list[4], 71), 0),
        "pattern": with_ends((jax.random.randint(key_list[3], (E, 6), 0, 4) < 3).astype(jnp.int32), jax.random.fold_in(key_list[3], 1), 0, 1),
    }


CENTER = 0.5
HALF_WIDTH = 2.0

def apply_hamiltonian(coeffs, hamiltonian, neighbours, pattern):
    count = E // LAYER

    def one_block(block_index):
        offset = block_index * LAYER
        own_block = lax.dynamic_slice_in_dim(coeffs, offset, LAYER, 0)
        linked = lax.dynamic_slice_in_dim(neighbours, offset, LAYER, 0)
        present = lax.dynamic_slice_in_dim(pattern, offset, LAYER, 0)
        hamilton = lax.dynamic_slice_in_dim(hamiltonian, offset, LAYER, 0)
        gathered = coeffs[linked] * present[:, :, None, None].astype(coeffs.dtype)
        stacked = jnp.concatenate([own_block[:, None], gathered], axis=1)
        stacked = stacked.reshape(LAYER, 7 * NB, NS)
        return jnp.einsum('eik,eks->eis', hamilton.astype(jnp.float32), stacked.astype(jnp.float32))
    result = lax.map(one_block, jnp.arange(count, dtype=jnp.int32))
    return result.reshape(E, NB, NS)

def reference(coefficients, hamiltonian, neighbours, pattern):
    start_block = coefficients.astype(jnp.float32)
    image_one = apply_hamiltonian(coefficients, hamiltonian, neighbours, pattern)
    filtered_one = ((image_one - CENTER * start_block) / HALF_WIDTH).astype(jnp.bfloat16)
    image_two = apply_hamiltonian(filtered_one, hamiltonian, neighbours, pattern)
    filtered_two = (2.0 * (image_two - CENTER * filtered_one.astype(jnp.float32)) / HALF_WIDTH - start_block).astype(jnp.bfloat16)
    matrix_rows = filtered_two.reshape(E * NB, NS)
    gram_matrix = lax.dot_general(matrix_rows.astype(jnp.float32), matrix_rows.astype(jnp.float32), (((0,), (0,)), ((), ())), preferred_element_type=jnp.float32)
    gram_matrix = gram_matrix / (E * NB)
    factor = jnp.linalg.cholesky(gram_matrix)
    identity = jnp.eye(NS, dtype=jnp.float32)
    rotation = lax.linalg.triangular_solve(factor, identity, left_side=True, lower=True, transpose_a=True).astype(jnp.bfloat16)
    result = jnp.dot(matrix_rows.astype(jnp.float32), rotation.astype(jnp.float32), preferred_element_type=jnp.float32).astype(jnp.bfloat16)
    return result.reshape(E, NB, NS)
```

```python
import functools

import jax
import jax.numpy as jnp
from jax import lax
from jax.experimental import pallas as pl
from jax.experimental.pallas import tpu as pltpu
from jax.sharding import PartitionSpec as P

LAYER = 32
CENTER = 0.5
HALF_WIDTH = 2.0
BLK = 128
BASE = 32
F32 = jnp.float32
BF16 = jnp.bfloat16
HIGHEST = lax.Precision.HIGHEST
MESH = pl.DeviceIdType.MESH
VMEM = pltpu.VMEM
MIB = 1024 * 1024


def in_vmem():
    return pl.BlockSpec(memory_space=pltpu.VMEM)


def in_smem():
    return pl.BlockSpec(memory_space=pltpu.SMEM)


def greet(devices):
    barrier = pltpu.get_barrier_semaphore()
    for device in devices:
        pl.semaphore_signal(barrier, inc=1, device_id=device, device_id_type=MESH)
    pl.semaphore_wait(barrier, len(devices))


def remote(src, dst, send, recv, device):
    return pltpu.make_async_remote_copy(
        src_ref=src, dst_ref=dst, send_sem=send, recv_sem=recv, device_id=device, device_id_type=MESH
    )


def filter_kernel(
    elems, states, nbr, pat, v_ref, h_ref, z_ref, g_ref,
    acc, f_ref, y_ref, tail_a, head_a, tail_b, head_b, halo_send, halo_recv, swap_send, swap_recv,
):
    count, basis, width = v_ref.shape
    rows = count * basis // states
    per = count // states
    me = lax.axis_index("elem")
    ms = lax.axis_index("state")
    right = lax.rem(me + 1, elems)
    left = lax.rem(me + elems - 1, elems)
    peers = [lax.rem(ms + d, states) for d in range(states)]
    greet([{"elem": right}, {"elem": left}] + [{"state": peers[d]} for d in range(1, states)])

    halo = ((tail_a, head_a), (tail_b, head_b))

    def exchange(stage, src):
        tail = remote(
            src.at[pl.ds(count - LAYER, LAYER)], halo[stage][0],
            halo_send.at[stage, 0], halo_recv.at[stage, 0], {"elem": right},
        )
        head = remote(
            src.at[pl.ds(0, LAYER)], halo[stage][1],
            halo_send.at[stage, 1], halo_recv.at[stage, 1], {"elem": left},
        )
        return tail, head

    def local_part(src):
        def body(e, carry):
            parts = [src[e]]
            for f in range(6):
                n = nbr[e, f]
                w = (pat[e, f] * (n // count == me).astype(jnp.int32)).astype(F32)
                parts.append(src[lax.rem(n, count)] * jnp.full((basis, width), w, F32).astype(BF16))
            stacked = jnp.concatenate(parts, axis=0)
            acc[e] = jnp.dot(h_ref[e], stacked, preferred_element_type=F32)
            return carry

        lax.fori_loop(0, count, body, 0, unroll=4)

    def image(stage, e, layer):
        face = 0 if layer == 1 else 1
        side = 1 if layer == 1 else 0
        w = pat[e, face].astype(F32)
        block = halo[stage][side][lax.rem(nbr[e, face], LAYER)]
        block = block * jnp.full((basis, width), w, F32).astype(BF16)
        strip = h_ref[e, :, (1 + face) * basis:(2 + face) * basis]
        return acc[e] + jnp.dot(strip, block, preferred_element_type=F32)

    first = exchange(0, v_ref)
    for c in first:
        c.start()
    local_part(v_ref)
    second = exchange(1, f_ref)
    for layer in range(2):
        first[layer].wait_recv()

        def one(i, carry):
            e = layer * LAYER + i
            f_ref[e] = ((image(0, e, layer) - CENTER * v_ref[e].astype(F32)) / HALF_WIDTH).astype(BF16)
            return carry

        lax.fori_loop(0, LAYER, one, 0, unroll=4)
        second[1 - layer].start()
    local_part(f_ref)
    swaps = [None] + [
        remote(
            y_ref.at[pl.ds(peers[d] * rows, rows)], z_ref.at[:, pl.ds(ms * width, width)],
            swap_send.at[d], swap_recv.at[d], {"state": peers[d]},
        )
        for d in range(1, states)
    ]
    for layer in range(2):
        second[layer].wait_recv()

        def two(i, carry):
            e = layer * LAYER + i
            out = 2.0 * (image(1, e, layer) - CENTER * f_ref[e].astype(F32)) / HALF_WIDTH
            y_ref[pl.ds(pl.multiple_of(e * basis, basis), basis), :] = (out - v_ref[e].astype(F32)).astype(BF16)
            return carry

        lax.fori_loop(0, LAYER, two, 0, unroll=4)
    for d in range(1, states):
        swaps[d].start()
    z_ref[:, pl.ds(pl.multiple_of(ms * width, width), width)] = y_ref[
        pl.ds(pl.multiple_of(ms * rows, rows), rows), :
    ]
    for c in first + second:
        c.wait_send()
    for d in range(1, states):
        swaps[d].wait()

    blocks = states * width // BLK
    offset = 0
    for k in range(blocks):
        strip = lax.dot_general(
            z_ref[:, k * BLK:(k + 1) * BLK], z_ref[:, k * BLK:], (((0,), (0,)), ((), ())),
            preferred_element_type=F32,
        )
        for j in range(blocks - k):
            g_ref[offset * BLK:(offset + 1) * BLK, :] = strip[:, j * BLK:(j + 1) * BLK]
            offset += 1


def filter_and_gram(coefficients, hamiltonian, neighbours, pattern, elems, states):
    count, basis, width = coefficients.shape
    rows = count * basis // states
    blocks = states * width // BLK
    packed = blocks * (blocks + 1) // 2 * BLK
    return pl.pallas_call(
        functools.partial(filter_kernel, elems, states),
        out_shape=(
            jax.ShapeDtypeStruct((rows, states * width), BF16),
            jax.ShapeDtypeStruct((packed, BLK), F32),
        ),
        in_specs=[in_smem(), in_smem(), in_vmem(), in_vmem()],
        out_specs=(in_vmem(), in_vmem()),
        scratch_shapes=[
            VMEM((count, basis, width), F32),
            VMEM((count, basis, width), BF16),
            VMEM((count * basis, width), BF16),
            VMEM((LAYER, basis, width), BF16),
            VMEM((LAYER, basis, width), BF16),
            VMEM((LAYER, basis, width), BF16),
            VMEM((LAYER, basis, width), BF16),
            pltpu.SemaphoreType.DMA((2, 2)),
            pltpu.SemaphoreType.DMA((2, 2)),
            pltpu.SemaphoreType.DMA((states,)),
            pltpu.SemaphoreType.DMA((states,)),
        ],
        compiler_params=pltpu.CompilerParams(
            collective_id=0, has_side_effects=True, vmem_limit_bytes=40 * MIB
        ),
        cost_estimate=pl.CostEstimate(flops=2 * 10**9, bytes_accessed=8 * MIB, transcendentals=0),
    )(neighbours, pattern, coefficients, hamiltonian)


SIZES = (4, 4, 8)


def sum_kernel(
    src, res, pair, acc, buf_a, buf_b, buf_c, core_send, core_recv, up_send, up_recv, down_send, down_recv,
):
    total = src.shape[0]
    half = total // 2
    part = half // 3
    me = lax.axis_index("elem")
    ms = lax.axis_index("state")
    core = lax.rem(me, 2)
    place = [lax.rem(ms, 4), (ms // 4) * 2 + me // 16, lax.rem(me, 16) // 2]

    def device(dim, at, c):
        spot = list(place)
        if dim is not None:
            spot[dim] = at
        x, y, z = spot
        return {"elem": lax.rem(y, 2) * 16 + z * 2 + c, "state": (y // 2) * 4 + x}

    def peer(dim, d):
        return lax.rem(place[dim] + d, SIZES[dim])

    other = device(None, None, 1 - core)
    greet([other] + [device(dim, peer(dim, d), core) for dim in range(3) for d in range(1, SIZES[dim])])

    mine = pl.multiple_of(core * half, 8)
    theirs = pl.multiple_of((1 - core) * half, 8)
    swap = remote(src.at[pl.ds(theirs, half)], pair, core_send.at[3], core_recv.at[3], other)
    swap.start()
    swap.wait()
    acc[...] = src[pl.ds(mine, half), :] + pair[...]

    orders = [[p % 3, (p + 1) % 3, (p + 2) % 3] for p in range(3)]
    len_a = [part // SIZES[o[0]] for o in orders]
    len_b = [len_a[p] // SIZES[orders[p][1]] for p in range(3)]
    base_a = [p * part + place[orders[p][0]] * len_a[p] for p in range(3)]
    base_b = [base_a[p] + place[orders[p][1]] * len_b[p] for p in range(3)]

    for level, buf in ((0, buf_a), (1, buf_b)):
        copies = [[] for _ in range(3)]
        for p in range(3):
            dim = orders[p][level]
            length = (len_a, len_b)[level][p]
            start = p * part if level == 0 else base_a[p]
            for d in range(1, SIZES[dim]):
                to = peer(dim, d)
                copies[p].append(
                    remote(
                        acc.at[pl.ds(pl.multiple_of(start + to * length, 8), length)],
                        buf.at[p, d, pl.ds(0, length)],
                        up_send.at[level, p, d], up_recv.at[level, p, d], device(dim, to, core),
                    )
                )
        for d in range(7):
            for p in range(3):
                if d < len(copies[p]):
                    copies[p][d].start()
        for p in range(3):
            dim = orders[p][level]
            length = (len_a, len_b)[level][p]
            start = p * part if level == 0 else base_a[p]
            own = pl.ds(pl.multiple_of(start + place[dim] * length, 8), length)
            total_rows = acc[own, :]
            for d in range(1, SIZES[dim]):
                copies[p][d - 1].wait_recv()
                total_rows = total_rows + buf[p, d, pl.ds(0, length), :]
            acc[own, :] = total_rows
        for p in range(3):
            for c in copies[p]:
                c.wait_send()

    copies = [[] for _ in range(3)]
    for p in range(3):
        dim = orders[p][2]
        length = len_b[p]
        spot = pl.ds(pl.multiple_of(base_b[p], 8), length)
        for d in range(1, SIZES[dim]):
            copies[p].append(
                remote(
                    acc.at[spot], buf_c.at[p, place[dim], pl.ds(0, length)],
                    up_send.at[2, p, d], up_recv.at[2, p, d], device(dim, peer(dim, d), core),
                )
            )
        buf_c[p, pl.ds(place[dim], 1), pl.ds(0, length), :] = acc[spot, :][None]
    for d in range(7):
        for p in range(3):
            if d < len(copies[p]):
                copies[p][d].start()
    for p in range(3):
        dim = orders[p][2]
        length = len_b[p]
        for c in copies[p]:
            c.wait_recv()
        total_rows = buf_c[p, 0, pl.ds(0, length), :]
        for i in range(1, SIZES[dim]):
            total_rows = total_rows + buf_c[p, i, pl.ds(0, length), :]
        res[pl.ds(pl.multiple_of(mine + base_b[p], 8), length), :] = total_rows
    for p in range(3):
        for c in copies[p]:
            c.wait_send()

    for level in (1, 0):
        copies = [[] for _ in range(3)]
        for p in range(3):
            dim = orders[p][level]
            length = (len_a, len_b)[level][p]
            start = (base_a, base_b)[level][p]
            spot = pl.ds(pl.multiple_of(mine + start, 8), length)
            for d in range(1, SIZES[dim]):
                copies[p].append(
                    remote(
                        res.at[spot], res.at[spot],
                        down_send.at[level, p, d], down_recv.at[level, p, d], device(dim, peer(dim, d), core),
                    )
                )
        for d in range(7):
            for p in range(3):
                if d < len(copies[p]):
                    copies[p][d].start()
        for p in range(3):
            for c in copies[p]:
                c.wait()
    last = []
    for p in range(3):
        spot = pl.ds(pl.multiple_of(mine + p * part, 8), part)
        last.append(remote(res.at[spot], res.at[spot], core_send.at[p], core_recv.at[p], other))
        last[p].start()
    for c in last:
        c.wait()


def sum_everywhere(packed):
    total = packed.shape[0]
    part = total // 6
    return pl.pallas_call(
        sum_kernel,
        out_shape=jax.ShapeDtypeStruct(packed.shape, F32),
        in_specs=[in_vmem()],
        out_specs=in_vmem(),
        scratch_shapes=[
            VMEM((total // 2, BLK), F32),
            VMEM((total // 2, BLK), F32),
            VMEM((3, 8, part // 4, BLK), F32),
            VMEM((3, 8, part // 16, BLK), F32),
            VMEM((3, 8, part // 16, BLK), F32),
            pltpu.SemaphoreType.DMA((4,)),
            pltpu.SemaphoreType.DMA((4,)),
            pltpu.SemaphoreType.DMA((3, 3, 8)),
            pltpu.SemaphoreType.DMA((3, 3, 8)),
            pltpu.SemaphoreType.DMA((2, 3, 8)),
            pltpu.SemaphoreType.DMA((2, 3, 8)),
        ],
        compiler_params=pltpu.CompilerParams(
            collective_id=1, has_side_effects=True, vmem_limit_bytes=40 * MIB
        ),
        cost_estimate=pl.CostEstimate(flops=10**7, bytes_accessed=5 * MIB, transcendentals=0),
    )(packed)


def tdot(a, b):
    return lax.dot_general(a, b, (((0,), (0,)), ((), ())), precision=HIGHEST, preferred_element_type=F32)


def base_step(p, tile):
    r0 = pl.multiple_of(p * BASE, BASE)
    panel = tile[pl.ds(r0, BASE), :]
    rolled = pltpu.roll(panel, lax.rem(BLK - r0, BLK), 1)
    lane = lax.broadcasted_iota(jnp.int32, (8, BLK), 1)
    sub = lax.broadcasted_iota(jnp.int32, (8, BLK), 0)
    groups = BASE // 8
    cols = [
        [jnp.broadcast_to(rolled[8 * g:8 * g + 8, k:k + 1], (8, BLK)) for g in range(groups)]
        for k in range(BASE)
    ]
    inside = (lane >= r0) & (lane < r0 + BASE)
    rows = [
        jnp.where(inside, (lane - r0 == sub + 8 * g).astype(F32), panel[8 * g:8 * g + 8])
        for g in range(groups)
    ]
    scales = [jnp.zeros((8, BLK), F32) for _ in range(groups)]
    for j in range(BASE):
        gj, sj = divmod(j, 8)
        pivot = jnp.broadcast_to(cols[j][gj][sj:sj + 1], (8, BLK))
        inverse = 1.0 / pivot
        scales[gj] = jnp.where(sub == sj, pivot, scales[gj])
        ratio = [None] * groups
        for g in range(gj, groups):
            ratio[g] = cols[j][g] * inverse
            if g == gj:
                ratio[g] = jnp.where(sub > sj, ratio[g], 0.0)
        for k in range(j + 1, BASE):
            row = jnp.broadcast_to(cols[k][gj][sj:sj + 1], (8, BLK))
            for g in range(gj, groups):
                if 8 * g + 7 > j:
                    cols[k][g] = cols[k][g] - ratio[g] * row
        row = jnp.broadcast_to(rows[gj][sj:sj + 1], (8, BLK))
        for g in range(gj, groups):
            if 8 * g + 7 > j:
                rows[g] = rows[g] - ratio[g] * row
    done = jnp.concatenate([rows[g] * lax.rsqrt(scales[g]) for g in range(groups)], axis=0)
    wide = lax.broadcasted_iota(jnp.int32, (BASE, BLK), 1)
    below = jnp.where(wide >= r0 + BASE, done, 0.0)
    update = tdot(below, done)
    rr = lax.broadcasted_iota(jnp.int32, (BLK, BLK), 0)
    cc = lax.broadcasted_iota(jnp.int32, (BLK, BLK), 1)
    clear = (rr >= r0 + BASE) & (cc >= r0) & (cc < r0 + BASE)
    tile[...] = jnp.where(clear, 0.0, tile[...]) - update
    tile[pl.ds(r0, BASE), :] = done


def inverse_kernel(n, scale, g_ref, x_ref, mat, tile):
    blocks = n // BLK
    offset = 0
    for k in range(blocks):
        for j in range(k, blocks):
            mat[k * BLK:(k + 1) * BLK, j * BLK:(j + 1) * BLK] = (
                g_ref[offset * BLK:(offset + 1) * BLK, :] * scale
            )
            offset += 1
    rr = lax.broadcasted_iota(jnp.int32, (BLK, BLK), 0)
    cc = lax.broadcasted_iota(jnp.int32, (BLK, BLK), 1)

    def step(k, carry):
        rows = pl.ds(pl.multiple_of(k * BLK, BLK), BLK)
        tile[...] = mat[rows, rows]

        def inner(p, c):
            base_step(p, tile)
            return c

        lax.fori_loop(0, BLK // BASE, inner, 0)
        corner = jnp.where(cc <= rr, tile[...], 0.0)
        mat[rows, rows] = (rr == cc).astype(F32)
        mat[rows, :] = jnp.dot(corner, mat[rows, :], precision=HIGHEST, preferred_element_type=F32)

        def update(i, c):
            at = pl.ds(pl.multiple_of(i * BLK, BLK), BLK)
            left = mat[rows, at]
            mat[at, rows] = jnp.zeros((BLK, BLK), F32)
            mat[at, :] = mat[at, :] - tdot(left, mat[rows, :])
            return c

        lax.fori_loop(k + 1, blocks, update, 0)
        return carry

    lax.fori_loop(0, blocks, step, 0)
    for k in range(blocks):
        for j in range(blocks):
            spot = (slice(k * BLK, (k + 1) * BLK), slice(j * BLK, (j + 1) * BLK))
            if j > k:
                x_ref[spot] = jnp.zeros((BLK, BLK), x_ref.dtype)
            elif j < k:
                x_ref[spot] = mat[spot].astype(x_ref.dtype)
            else:
                x_ref[spot] = jnp.where(cc <= rr, mat[spot], 0.0).astype(x_ref.dtype)


def inverse_factor(packed, n, scale):
    return pl.pallas_call(
        functools.partial(inverse_kernel, n, scale),
        out_shape=jax.ShapeDtypeStruct((n, n), BF16),
        in_specs=[in_vmem()],
        out_specs=in_vmem(),
        scratch_shapes=[VMEM((n, n), F32), VMEM((BLK, BLK), F32)],
        compiler_params=pltpu.CompilerParams(vmem_limit_bytes=40 * MIB),
        cost_estimate=pl.CostEstimate(flops=6 * n**3, bytes_accessed=4 * n * n, transcendentals=0),
    )(packed)


def rotate_kernel(states, z_ref, x_ref, o_ref, out, send, recv):
    rows, n = z_ref.shape
    width = n // states
    ms = lax.axis_index("state")
    peers = [lax.rem(ms + d, states) for d in range(states)]
    greet([{"state": peers[d]} for d in range(1, states)])
    mine = pl.ds(pl.multiple_of(ms * rows, rows), rows)
    copies = []
    for d in list(range(1, states)) + [0]:
        at = pl.ds(pl.multiple_of(peers[d] * width, width), width)
        block = lax.dot_general(
            z_ref[...], x_ref[at, :], (((1,), (1,)), ((), ())), preferred_element_type=F32
        ).astype(BF16)
        if d == 0:
            o_ref[mine, :] = block
        else:
            out[d] = block
            copies.append(remote(out.at[d], o_ref.at[mine], send.at[d], recv.at[d], {"state": peers[d]}))
            copies[-1].start()
    for c in copies:
        c.wait()


def rotate(rows, inverse, states):
    count, n = rows.shape
    width = n // states
    return pl.pallas_call(
        functools.partial(rotate_kernel, states),
        out_shape=jax.ShapeDtypeStruct((count * states, width), BF16),
        in_specs=[in_vmem(), in_vmem()],
        out_specs=in_vmem(),
        scratch_shapes=[
            VMEM((states, count, width), BF16),
            pltpu.SemaphoreType.DMA((states,)),
            pltpu.SemaphoreType.DMA((states,)),
        ],
        compiler_params=pltpu.CompilerParams(
            collective_id=2, has_side_effects=True, vmem_limit_bytes=40 * MIB
        ),
        cost_estimate=pl.CostEstimate(flops=2 * count * n * n, bytes_accessed=4 * MIB, transcendentals=0),
    )(rows, inverse)


def on_device(coefficients, hamiltonian, neighbours, pattern):
    count, basis, width = coefficients.shape
    elems = lax.axis_size("elem")
    states = lax.axis_size("state")
    rows, gram = filter_and_gram(coefficients, hamiltonian, neighbours, pattern, elems, states)
    gram = sum_everywhere(gram)
    inverse = inverse_factor(gram, states * width, 1.0 / (count * elems * basis))
    result = rotate(rows, inverse, states)
    return result.reshape(count, basis, width)


def solution(mesh):
    return jax.shard_map(
        on_device,
        mesh=mesh,
        in_specs=(
            P("elem", None, "state"),
            P("elem", None, None),
            P("elem", None),
            P("elem", None),
        ),
        out_specs=P("elem", None, "state"),
        check_vma=False,
    )
```

```python
import functools

import jax
import jax.numpy as jnp
from jax import lax
from jax.experimental import pallas as pl
from jax.experimental.pallas import tpu as pltpu
from jax.sharding import PartitionSpec as P

LAYER = 32
CENTER = 0.5
HALF_WIDTH = 2.0
BLK = 128
BASE = 32
F32 = jnp.float32
BF16 = jnp.bfloat16
MESH = pl.DeviceIdType.MESH
VMEM = pltpu.VMEM
MIB = 1024 * 1024


def in_vmem():
    return pl.BlockSpec(memory_space=pltpu.VMEM)


def in_hbm():
    return pl.BlockSpec(memory_space=pl.ANY)


def in_smem():
    return pl.BlockSpec(memory_space=pltpu.SMEM)


def greet(devices):
    barrier = pltpu.get_barrier_semaphore()
    for device in devices:
        pl.semaphore_signal(barrier, inc=1, device_id=device, device_id_type=MESH)
    pl.semaphore_wait(barrier, len(devices))


def remote(src, dst, send, recv, device):
    return pltpu.make_async_remote_copy(
        src_ref=src, dst_ref=dst, send_sem=send, recv_sem=recv, device_id=device, device_id_type=MESH
    )


def filter_kernel(
    elems, states, nbr, pat, v_hbm, h_hbm, z_ref, g_ref,
    v_ref, h_ref, load, acc, f_ref, y_ref, tail_a, head_a, tail_b, head_b, halo_send, halo_recv, swap_send, swap_recv,
):
    count, basis, width = v_ref.shape
    rows = count * basis // states
    per = count // states
    me = lax.axis_index("elem")
    ms = lax.axis_index("state")
    right = lax.rem(me + 1, elems)
    left = lax.rem(me + elems - 1, elems)
    peers = [lax.rem(ms + d, states) for d in range(states)]
    load_v = pltpu.make_async_copy(v_hbm, v_ref, load.at[0])
    load_h = pltpu.make_async_copy(h_hbm, h_ref, load.at[1])
    load_v.start()
    load_h.start()
    greet([{"elem": right}, {"elem": left}] + [{"state": peers[d]} for d in range(1, states)])

    halo = ((tail_a, head_a), (tail_b, head_b))

    def exchange(stage, src):
        tail = remote(
            src.at[pl.ds(count - LAYER, LAYER)], halo[stage][0],
            halo_send.at[stage, 0], halo_recv.at[stage, 0], {"elem": right},
        )
        head = remote(
            src.at[pl.ds(0, LAYER)], halo[stage][1],
            halo_send.at[stage, 1], halo_recv.at[stage, 1], {"elem": left},
        )
        return tail, head

    def local_part(src):
        def body(e, carry):
            parts = [src[e]]
            for f in range(6):
                n = nbr[f, e]
                w = (pat[f, e] * (n // count == me).astype(jnp.int32)).astype(F32)
                parts.append(src[lax.rem(n, count)] * jnp.full((basis, width), w, F32).astype(BF16))
            stacked = jnp.concatenate(parts, axis=0)
            acc[e] = jnp.dot(h_ref[e], stacked, preferred_element_type=F32)
            return carry

        lax.fori_loop(0, count, body, 0, unroll=4)

    def image(stage, e, layer):
        face = 0 if layer == 1 else 1
        side = 1 if layer == 1 else 0
        w = pat[face, e].astype(F32)
        block = halo[stage][side][lax.rem(nbr[face, e], LAYER)]
        block = block * jnp.full((basis, width), w, F32).astype(BF16)
        strip = h_ref[e, :, (1 + face) * basis:(2 + face) * basis]
        return acc[e] + jnp.dot(strip, block, preferred_element_type=F32)

    load_v.wait()
    first = exchange(0, v_ref)
    for c in first:
        c.start()
    load_h.wait()
    local_part(v_ref)
    second = exchange(1, f_ref)
    for layer in range(2):
        first[layer].wait_recv()

        def one(i, carry):
            e = layer * LAYER + i
            f_ref[e] = ((image(0, e, layer) - CENTER * v_ref[e].astype(F32)) / HALF_WIDTH).astype(BF16)
            return carry

        lax.fori_loop(0, LAYER, one, 0, unroll=4)
        second[1 - layer].start()
    local_part(f_ref)
    swaps = [None] + [
        remote(
            y_ref.at[pl.ds(peers[d] * rows, rows)], z_ref.at[:, pl.ds(ms * width, width)],
            swap_send.at[d], swap_recv.at[d], {"state": peers[d]},
        )
        for d in range(1, states)
    ]
    for layer in range(2):
        second[layer].wait_recv()

        def two(i, carry):
            e = layer * LAYER + i
            out = 2.0 * (image(1, e, layer) - CENTER * f_ref[e].astype(F32)) / HALF_WIDTH
            y_ref[pl.ds(pl.multiple_of(e * basis, basis), basis), :] = (out - v_ref[e].astype(F32)).astype(BF16)
            return carry

        lax.fori_loop(0, LAYER, two, 0, unroll=4)
    for d in range(1, states):
        swaps[d].start()
    z_ref[:, pl.ds(pl.multiple_of(ms * width, width), width)] = y_ref[
        pl.ds(pl.multiple_of(ms * rows, rows), rows), :
    ]
    for c in first + second:
        c.wait_send()
    for d in range(1, states):
        swaps[d].wait()

    blocks = states * width // BLK
    offset = 0
    for k in range(blocks):
        strip = lax.dot_general(
            z_ref[:, k * BLK:(k + 1) * BLK], z_ref[:, k * BLK:], (((0,), (0,)), ((), ())),
            preferred_element_type=F32,
        )
        for j in range(blocks - k):
            g_ref[offset * BLK:(offset + 1) * BLK, :] = strip[:, j * BLK:(j + 1) * BLK]
            offset += 1


def filter_and_gram(coefficients, hamiltonian, neighbours, pattern, elems, states):
    count, basis, width = coefficients.shape
    rows = count * basis // states
    blocks = states * width // BLK
    packed = blocks * (blocks + 1) // 2 * BLK
    return pl.pallas_call(
        functools.partial(filter_kernel, elems, states),
        out_shape=(
            jax.ShapeDtypeStruct((rows, states * width), BF16),
            jax.ShapeDtypeStruct((packed, BLK), F32),
        ),
        in_specs=[in_smem(), in_smem(), in_hbm(), in_hbm()],
        out_specs=(in_vmem(), in_vmem()),
        scratch_shapes=[
            VMEM(coefficients.shape, BF16),
            VMEM(hamiltonian.shape, BF16),
            pltpu.SemaphoreType.DMA((2,)),
            VMEM((count, basis, width), F32),
            VMEM((count, basis, width), BF16),
            VMEM((count * basis, width), BF16),
            VMEM((LAYER, basis, width), BF16),
            VMEM((LAYER, basis, width), BF16),
            VMEM((LAYER, basis, width), BF16),
            VMEM((LAYER, basis, width), BF16),
            pltpu.SemaphoreType.DMA((2, 2)),
            pltpu.SemaphoreType.DMA((2, 2)),
            pltpu.SemaphoreType.DMA((states,)),
            pltpu.SemaphoreType.DMA((states,)),
        ],
        compiler_params=pltpu.CompilerParams(
            collective_id=0, has_side_effects=True, vmem_limit_bytes=40 * MIB
        ),
        cost_estimate=pl.CostEstimate(flops=2 * 10**9, bytes_accessed=8 * MIB, transcendentals=0),
    )(neighbours.T, pattern.T, coefficients, hamiltonian)


SIZES = (4, 4, 8)


def sum_kernel(
    src, res, pair, acc, buf_a, buf_b, buf_c, core_send, core_recv, up_send, up_recv, down_send, down_recv,
):
    total = src.shape[0]
    half = total // 2
    part = half // 3
    me = lax.axis_index("elem")
    ms = lax.axis_index("state")
    core = lax.rem(me, 2)
    place = [lax.rem(ms, 4), (ms // 4) * 2 + me // 16, lax.rem(me, 16) // 2]

    def device(dim, at, c):
        spot = list(place)
        if dim is not None:
            spot[dim] = at
        x, y, z = spot
        return {"elem": lax.rem(y, 2) * 16 + z * 2 + c, "state": (y // 2) * 4 + x}

    def peer(dim, d):
        return lax.rem(place[dim] + d, SIZES[dim])

    other = device(None, None, 1 - core)
    greet([other] + [device(dim, peer(dim, d), core) for dim in range(3) for d in range(1, SIZES[dim])])

    mine = pl.multiple_of(core * half, 8)
    theirs = pl.multiple_of((1 - core) * half, 8)
    swap = remote(src.at[pl.ds(theirs, half)], pair, core_send.at[3], core_recv.at[3], other)
    swap.start()
    swap.wait()
    acc[...] = src[pl.ds(mine, half), :] + pair[...]

    orders = [[p % 3, (p + 1) % 3, (p + 2) % 3] for p in range(3)]
    len_a = [part // SIZES[o[0]] for o in orders]
    len_b = [len_a[p] // SIZES[orders[p][1]] for p in range(3)]
    base_a = [p * part + place[orders[p][0]] * len_a[p] for p in range(3)]
    base_b = [base_a[p] + place[orders[p][1]] * len_b[p] for p in range(3)]

    for level, buf in ((0, buf_a), (1, buf_b)):
        copies = [[] for _ in range(3)]
        for p in range(3):
            dim = orders[p][level]
            length = (len_a, len_b)[level][p]
            start = p * part if level == 0 else base_a[p]
            for d in range(1, SIZES[dim]):
                to = peer(dim, d)
                copies[p].append(
                    remote(
                        acc.at[pl.ds(pl.multiple_of(start + to * length, 8), length)],
                        buf.at[p, d, pl.ds(0, length)],
                        up_send.at[level, p, d], up_recv.at[level, p, d], device(dim, to, core),
                    )
                )
        for d in range(7):
            for p in range(3):
                if d < len(copies[p]):
                    copies[p][d].start()
        for p in range(3):
            dim = orders[p][level]
            length = (len_a, len_b)[level][p]
            start = p * part if level == 0 else base_a[p]
            own = pl.ds(pl.multiple_of(start + place[dim] * length, 8), length)
            total_rows = acc[own, :]
            for d in range(1, SIZES[dim]):
                copies[p][d - 1].wait_recv()
                total_rows = total_rows + buf[p, d, pl.ds(0, length), :]
            acc[own, :] = total_rows
        for p in range(3):
            for c in copies[p]:
                c.wait_send()

    copies = [[] for _ in range(3)]
    for p in range(3):
        dim = orders[p][2]
        length = len_b[p]
        spot = pl.ds(pl.multiple_of(base_b[p], 8), length)
        for d in range(1, SIZES[dim]):
            copies[p].append(
                remote(
                    acc.at[spot], buf_c.at[p, place[dim], pl.ds(0, length)],
                    up_send.at[2, p, d], up_recv.at[2, p, d], device(dim, peer(dim, d), core),
                )
            )
        buf_c[p, pl.ds(place[dim], 1), pl.ds(0, length), :] = acc[spot, :][None]
    for d in range(7):
        for p in range(3):
            if d < len(copies[p]):
                copies[p][d].start()
    for p in range(3):
        dim = orders[p][2]
        length = len_b[p]
        for c in copies[p]:
            c.wait_recv()
        total_rows = buf_c[p, 0, pl.ds(0, length), :]
        for i in range(1, SIZES[dim]):
            total_rows = total_rows + buf_c[p, i, pl.ds(0, length), :]
        res[pl.ds(pl.multiple_of(mine + base_b[p], 8), length), :] = total_rows
    for p in range(3):
        for c in copies[p]:
            c.wait_send()

    for level in (1, 0):
        copies = [[] for _ in range(3)]
        for p in range(3):
            dim = orders[p][level]
            length = (len_a, len_b)[level][p]
            start = (base_a, base_b)[level][p]
            spot = pl.ds(pl.multiple_of(mine + start, 8), length)
            for d in range(1, SIZES[dim]):
                copies[p].append(
                    remote(
                        res.at[spot], res.at[spot],
                        down_send.at[level, p, d], down_recv.at[level, p, d], device(dim, peer(dim, d), core),
                    )
                )
        for d in range(7):
            for p in range(3):
                if d < len(copies[p]):
                    copies[p][d].start()
        for p in range(3):
            for c in copies[p]:
                c.wait()
    last = []
    for p in range(3):
        spot = pl.ds(pl.multiple_of(mine + p * part, 8), part)
        last.append(remote(res.at[spot], res.at[spot], core_send.at[p], core_recv.at[p], other))
        last[p].start()
    for c in last:
        c.wait()


def sum_everywhere(packed):
    total = packed.shape[0]
    part = total // 6
    return pl.pallas_call(
        sum_kernel,
        out_shape=jax.ShapeDtypeStruct(packed.shape, F32),
        in_specs=[in_vmem()],
        out_specs=in_vmem(),
        scratch_shapes=[
            VMEM((total // 2, BLK), F32),
            VMEM((total // 2, BLK), F32),
            VMEM((3, 8, part // 4, BLK), F32),
            VMEM((3, 8, part // 16, BLK), F32),
            VMEM((3, 8, part // 16, BLK), F32),
            pltpu.SemaphoreType.DMA((4,)),
            pltpu.SemaphoreType.DMA((4,)),
            pltpu.SemaphoreType.DMA((3, 3, 8)),
            pltpu.SemaphoreType.DMA((3, 3, 8)),
            pltpu.SemaphoreType.DMA((2, 3, 8)),
            pltpu.SemaphoreType.DMA((2, 3, 8)),
        ],
        compiler_params=pltpu.CompilerParams(
            collective_id=1, has_side_effects=True, vmem_limit_bytes=40 * MIB
        ),
        cost_estimate=pl.CostEstimate(flops=10**7, bytes_accessed=5 * MIB, transcendentals=0),
    )(packed)


def recip(x):
    q = pl.reciprocal(x, approx=True)
    return q * (2.0 - x * q)


def split(x):
    h = x.astype(BF16)
    r = x - h.astype(F32)
    m = r.astype(BF16)
    return h, m, (r - m.astype(F32)).astype(BF16)


def left_stack(x):
    h, m, l = split(x)
    return jnp.concatenate([h, h, m, h, m, l], axis=0)


def right_stack(x):
    h, m, l = split(x)
    return jnp.concatenate([h, m, h, l, m, h], axis=0)


def sdot(a, b):
    return lax.dot_general(a, b, (((0,), (0,)), ((), ())), preferred_element_type=F32)


def base_step(p, panel):
    r0 = p * BASE
    lane = lax.broadcasted_iota(jnp.int32, (8, BLK), 1)
    sub = lax.broadcasted_iota(jnp.int32, (8, BLK), 0)
    groups = BASE // 8
    rows = [panel[8 * g:8 * g + 8] for g in range(groups)]
    cols = [
        {g: jnp.broadcast_to(rows[g][:, r0 + k:r0 + k + 1], (8, BLK)) for g in range(k // 8, groups)}
        for k in range(BASE)
    ]
    inside = (lane >= r0) & (lane < r0 + BASE)
    rows = [
        jnp.where(inside, (lane - r0 == sub + 8 * g).astype(F32), rows[g]) for g in range(groups)
    ]
    scales = [jnp.ones((8, BLK), F32) for _ in range(groups)]

    def at(vecs, i):
        return jnp.broadcast_to(vecs[i // 8][i % 8:i % 8 + 1], (8, BLK))

    for j in range(0, BASE, 2):
        gj, sj = divmod(j, 8)
        a, b, d = at(cols[j], j), at(cols[j], j + 1), at(cols[j + 1], j + 1)
        det = a * d - b * b
        ra = recip(a)
        rdet = recip(det)
        slope = b * ra
        inv = a * rdet
        scales[gj] = jnp.where(sub == sj, a, jnp.where(sub == sj + 1, det * ra, scales[gj]))
        first, reduced, second = {}, {}, {}
        for g in range(gj, groups):
            c = cols[j][g]
            first[g] = c * ra
            reduced[g] = cols[j + 1][g] - c * slope
            second[g] = reduced[g] * inv
            if g == gj:
                first[g] = jnp.where(sub > sj + 1, first[g], 0.0)
                second[g] = jnp.where(sub > sj + 1, second[g], 0.0)
        for k in range(j + 2, BASE):
            low, high = at(cols[j], k), at(reduced, k)
            for g in range(k // 8, groups):
                cols[k][g] = cols[k][g] - first[g] * low - second[g] * high
        low = at(rows, j)
        high = at(rows, j + 1) - slope * low
        rows[gj] = jnp.where(sub == sj + 1, high, rows[gj])
        for g in range(gj, groups):
            if 8 * g + 7 > j + 1:
                rows[g] = rows[g] - first[g] * low - second[g] * high
    return jnp.concatenate([rows[g] * lax.rsqrt(scales[g]) for g in range(groups)], axis=0)


def factor_block(block, aside):
    rr = lax.broadcasted_iota(jnp.int32, (BLK, BLK), 0)
    cc = lax.broadcasted_iota(jnp.int32, (BLK, BLK), 1)
    diagonal = jnp.where(rr == cc, block, 0.0)
    across = lax.rsqrt(jnp.sum(diagonal, axis=0, keepdims=True))
    down = lax.rsqrt(jnp.sum(diagonal, axis=1, keepdims=True))
    rest = block * across * down
    parts = []
    for p in range(BLK // BASE):
        aside(p)
        done = base_step(p, rest[:BASE])
        parts.append(done)
        if p + 1 < BLK // BASE:
            r1 = (p + 1) * BASE
            lane = lax.broadcasted_iota(jnp.int32, (BLK - r1, BLK), 1)
            update = sdot(left_stack(done)[:, r1:], right_stack(done))
            rest = jnp.where((lane >= r1 - BASE) & (lane < r1), 0.0, rest[BASE:]) - update
    return jnp.where(cc <= rr, jnp.concatenate(parts, axis=0), 0.0) * across


def rotate_kernel(states, scale, g_ref, z_ref, o_ref, mat, left, right, out, send, recv):
    rows, n = z_ref.shape
    blocks = n // BLK
    ms = lax.axis_index("state")
    greet([{"state": lax.rem(ms + d, states)} for d in range(1, states)])
    mine = pl.ds(pl.multiple_of(ms * rows, rows), rows)

    def hand_over(t):
        return remote(out.at[t], o_ref.at[mine], send.at[t], recv.at[ms], {"state": t})

    def rotate_block(t):
        strip = mat[at[t], :(t + 1) * BLK].astype(BF16)
        block = lax.dot_general(
            z_ref[:, :(t + 1) * BLK], strip, (((1,), (1,)), ((), ())), preferred_element_type=F32
        ).astype(BF16)

        @pl.when(ms == t)
        def _():
            o_ref[mine, :] = block

        @pl.when(ms != t)
        def _():
            out[t] = block
            hand_over(t).start()

    at = [pl.ds(k * BLK, BLK) for k in range(blocks)]
    offset = 0
    for k in range(blocks):
        for j in range(k, blocks):
            mat[at[k], at[j]] = g_ref[pl.ds(offset * BLK, BLK), :] * scale
            offset += 1

    def apply(k, i, diagonal):
        slot = k % 2
        if diagonal:
            mat[at[i], at[i]] = mat[at[i], at[i]] - sdot(left[slot, :, at[i]], right[slot, :, at[i]])
            return
        lhs = left[slot, :, at[i]]
        old = pl.ds(0, (k + 1) * BLK)
        change = sdot(lhs, right[slot, :, old])
        if k > 0:
            done = pl.ds(0, k * BLK)
            mat[at[i], done] = mat[at[i], done] - change[:, :k * BLK]
        mat[at[i], at[k]] = -change[:, k * BLK:]
        first = i + 1 if i == k + 1 else i
        if first < blocks:
            new = pl.ds(first * BLK, (blocks - first) * BLK)
            mat[at[i], new] = mat[at[i], new] - sdot(lhs, right[slot, :, new])

    for k in range(blocks):
        def aside(p, k=k):
            if k > 0:
                todo = list(range(k, blocks))
                for i in todo[p::BLK // BASE]:
                    apply(k - 1, i, False)

        corner = factor_block(mat[at[k], at[k]], aside)
        mat[at[k], at[k]] = corner
        lhs = left_stack(corner.T)
        slot = k % 2
        pieces = []
        if k > 0:
            done = pl.ds(0, k * BLK)
            pieces.append((done, sdot(lhs, right_stack(mat[at[k], done]))))
        if k + 1 < blocks:
            new = pl.ds((k + 1) * BLK, (blocks - k - 1) * BLK)
            pieces.append((new, sdot(lhs, right_stack(mat[at[k], new]))))
            right[slot, :, at[k]] = right_stack(corner)
        for where, piece in pieces:
            mat[at[k], where] = piece
            if k + 1 < blocks:
                right[slot, :, where] = right_stack(piece)
        if k + 1 < blocks:
            left[slot, :, new] = left_stack(pieces[-1][1])
            apply(k, k + 1, True)
        rotate_block(k)
    for t in range(states):

        @pl.when(ms != t)
        def _():
            hand_over(t).wait_send()
            rows_of = o_ref.at[pl.ds(t * rows, rows)]
            remote(out.at[t], rows_of, send.at[t], recv.at[t], {"state": t}).wait_recv()


def rotate(gram, rows, scale, states):
    count, n = rows.shape
    width = n // states
    return pl.pallas_call(
        functools.partial(rotate_kernel, states, scale),
        out_shape=jax.ShapeDtypeStruct((count * states, width), BF16),
        in_specs=[in_vmem(), in_vmem()],
        out_specs=in_vmem(),
        scratch_shapes=[
            VMEM((n, n), F32),
            VMEM((2, 6 * BLK, n), BF16),
            VMEM((2, 6 * BLK, n), BF16),
            VMEM((states, count, width), BF16),
            pltpu.SemaphoreType.DMA((states,)),
            pltpu.SemaphoreType.DMA((states,)),
        ],
        compiler_params=pltpu.CompilerParams(
            collective_id=2, has_side_effects=True, vmem_limit_bytes=48 * MIB
        ),
        cost_estimate=pl.CostEstimate(flops=2 * count * n * n + 6 * n**3, bytes_accessed=4 * MIB, transcendentals=0),
    )(gram, rows)


def on_device(coefficients, hamiltonian, neighbours, pattern):
    count, basis, width = coefficients.shape
    elems = lax.axis_size("elem")
    states = lax.axis_size("state")
    rows, gram = filter_and_gram(coefficients, hamiltonian, neighbours, pattern, elems, states)
    gram = sum_everywhere(gram)
    result = rotate(gram, rows, 1.0 / (count * elems * basis), states)
    return result.reshape(count, basis, width)


def solution(mesh):
    return jax.shard_map(
        on_device,
        mesh=mesh,
        in_specs=(
            P("elem", None, "state"),
            P("elem", None, None),
            P("elem", None),
            P("elem", None),
        ),
        out_specs=P("elem", None, "state"),
        check_vma=False,
    )
```

```python
import functools

import jax
import jax.numpy as jnp
from jax import lax
from jax.experimental import pallas as pl
from jax.experimental.pallas import tpu as pltpu
from jax.sharding import PartitionSpec as P

LAYER = 32
CENTER = 0.5
HALF_WIDTH = 2.0
BLK = 128
BASE = 32
F32 = jnp.float32
BF16 = jnp.bfloat16
MESH = pl.DeviceIdType.MESH
VMEM = pltpu.VMEM
MIB = 1024 * 1024


def in_vmem():
    return pl.BlockSpec(memory_space=pltpu.VMEM)


def in_hbm():
    return pl.BlockSpec(memory_space=pl.ANY)


def in_smem():
    return pl.BlockSpec(memory_space=pltpu.SMEM)


def greet(devices):
    barrier = pltpu.get_barrier_semaphore()
    for device in devices:
        pl.semaphore_signal(barrier, inc=1, device_id=device, device_id_type=MESH)
    pl.semaphore_wait(barrier, len(devices))


def remote(src, dst, send, recv, device):
    return pltpu.make_async_remote_copy(
        src_ref=src, dst_ref=dst, send_sem=send, recv_sem=recv, device_id=device, device_id_type=MESH
    )


def recip(x):
    q = pl.reciprocal(x, approx=True)
    return q * (2.0 - x * q)


def split(x):
    h = x.astype(BF16)
    r = x - h.astype(F32)
    m = r.astype(BF16)
    return h, m, (r - m.astype(F32)).astype(BF16)


def left_stack(x):
    h, m, l = split(x)
    return jnp.concatenate([h, h, m, h, m, l], axis=0)


def right_stack(x):
    h, m, l = split(x)
    return jnp.concatenate([h, m, h, l, m, h], axis=0)


def sdot(a, b):
    return lax.dot_general(a, b, (((0,), (0,)), ((), ())), preferred_element_type=F32)


def base_step(p, panel):
    r0 = p * BASE
    lane = lax.broadcasted_iota(jnp.int32, (8, BLK), 1)
    sub = lax.broadcasted_iota(jnp.int32, (8, BLK), 0)
    groups = BASE // 8
    rows = [panel[8 * g:8 * g + 8] for g in range(groups)]
    cols = [
        {g: jnp.broadcast_to(rows[g][:, r0 + k:r0 + k + 1], (8, BLK)) for g in range(k // 8, groups)}
        for k in range(BASE)
    ]
    inside = (lane >= r0) & (lane < r0 + BASE)
    rows = [
        jnp.where(inside, (lane - r0 == sub + 8 * g).astype(F32), rows[g]) for g in range(groups)
    ]
    scales = [jnp.ones((8, BLK), F32) for _ in range(groups)]

    def at(vecs, i):
        return jnp.broadcast_to(vecs[i // 8][i % 8:i % 8 + 1], (8, BLK))

    for j in range(0, BASE, 2):
        gj, sj = divmod(j, 8)
        a, b, d = at(cols[j], j), at(cols[j], j + 1), at(cols[j + 1], j + 1)
        det = a * d - b * b
        ra = recip(a)
        rdet = recip(det)
        slope = b * ra
        inv = a * rdet
        scales[gj] = jnp.where(sub == sj, a, jnp.where(sub == sj + 1, det * ra, scales[gj]))
        first, reduced, second = {}, {}, {}
        for g in range(gj, groups):
            c = cols[j][g]
            first[g] = c * ra
            reduced[g] = cols[j + 1][g] - c * slope
            second[g] = reduced[g] * inv
            if g == gj:
                first[g] = jnp.where(sub > sj + 1, first[g], 0.0)
                second[g] = jnp.where(sub > sj + 1, second[g], 0.0)
        for k in range(j + 2, BASE):
            low, high = at(cols[j], k), at(reduced, k)
            for g in range(k // 8, groups):
                cols[k][g] = cols[k][g] - first[g] * low - second[g] * high
        low = at(rows, j)
        high = at(rows, j + 1) - slope * low
        rows[gj] = jnp.where(sub == sj + 1, high, rows[gj])
        for g in range(gj, groups):
            if 8 * g + 7 > j + 1:
                rows[g] = rows[g] - first[g] * low - second[g] * high
    return jnp.concatenate([rows[g] * lax.rsqrt(scales[g]) for g in range(groups)], axis=0)


def factor_block(block, aside):
    rr = lax.broadcasted_iota(jnp.int32, (BLK, BLK), 0)
    cc = lax.broadcasted_iota(jnp.int32, (BLK, BLK), 1)
    diagonal = jnp.where(rr == cc, block, 0.0)
    across = lax.rsqrt(jnp.sum(diagonal, axis=0, keepdims=True))
    down = lax.rsqrt(jnp.sum(diagonal, axis=1, keepdims=True))
    rest = block * across * down
    parts = []
    for p in range(BLK // BASE):
        aside(p)
        done = base_step(p, rest[:BASE])
        parts.append(done)
        if p + 1 < BLK // BASE:
            r1 = (p + 1) * BASE
            lane = lax.broadcasted_iota(jnp.int32, (BLK - r1, BLK), 1)
            update = sdot(left_stack(done)[:, r1:], right_stack(done))
            rest = jnp.where((lane >= r1 - BASE) & (lane < r1), 0.0, rest[BASE:]) - update
    return jnp.where(cc <= rr, jnp.concatenate(parts, axis=0), 0.0) * across


FIRST = (
    [(0, j) for j in range(8)],
    [(1, j) for j in range(1, 8)] + [(2, 2)],
)
SECOND = (
    [(2, j) for j in range(3, 8)] + [(3, j) for j in range(3, 8)],
    [(i, j) for i in range(4, 8) for j in range(i, 8)],
)
HALF = (len(FIRST[0]) + len(SECOND[0])) * BLK
STREAM_ROWS = (len(FIRST[0]) * BLK, len(SECOND[0]) * BLK)
STREAM_AT = (0, STREAM_ROWS[0])
SIZES = (4, 4, 8)
TILE = 8
WIDE = STREAM_ROWS[1] // 8


def packed_blocks():
    return FIRST[0] + SECOND[0] + FIRST[1] + SECOND[1]


def runs(pairs):
    found = []
    for i, j in pairs:
        if found and found[-1][0] == i and found[-1][1] + found[-1][2] == j:
            found[-1][2] += 1
        else:
            found.append([i, j, 1])
    return found


def whole_kernel(
    elems, states, scale, nbr, pat, v_hbm, h_hbm, o_ref,
    z_ref, res, mat, left_terms, right_terms, out, send, recv,
    v_ref, h_ref, load, acc, f_ref, y_ref, tail_a, head_a, tail_b, head_b,
    halo_send, halo_recv, swap_send, swap_recv,
    gram, pair, buf_a, buf_b, buf_c, buf_d,
    core_send, core_recv, up_send, up_recv, down_send, down_recv,
):
    count, basis, width = v_ref.shape
    rows = count * basis // states
    per = count // states
    me = lax.axis_index("elem")
    ms = lax.axis_index("state")
    right = lax.rem(me + 1, elems)
    left = lax.rem(me + elems - 1, elems)
    core = lax.rem(me, 2)
    place = [lax.rem(ms, 4), (ms // 4) * 2 + me // 16, lax.rem(me, 16) // 2]

    def device(dim, at, c):
        spot = list(place)
        if dim is not None:
            spot[dim] = at
        x, y, z = spot
        return {"elem": lax.rem(y, 2) * 16 + z * 2 + c, "state": (y // 2) * 4 + x}

    def peer(dim, d):
        return lax.rem(place[dim] + d, SIZES[dim])

    load_v = pltpu.make_async_copy(v_hbm, v_ref, load.at[0])
    load_h = pltpu.make_async_copy(h_hbm, h_ref, load.at[1])
    load_v.start()
    load_h.start()
    greet(
        [{"elem": right}, {"elem": left}]
        + [{"state": lax.rem(ms + d, states)} for d in range(1, states)]
        + [device(1, peer(1, d), core) for d in (1, 3)]
        + [device(2, peer(2, d), core) for d in range(1, 8)]
    )

    halo = ((tail_a, head_a), (tail_b, head_b))

    def exchange(stage, src):
        tail = remote(
            src.at[pl.ds(count - LAYER, LAYER)], halo[stage][0],
            halo_send.at[stage, 0], halo_recv.at[stage, 0], {"elem": right},
        )
        head = remote(
            src.at[pl.ds(0, LAYER)], halo[stage][1],
            halo_send.at[stage, 1], halo_recv.at[stage, 1], {"elem": left},
        )
        return tail, head

    def local_part(src):
        def body(e, carry):
            parts = [src[e]]
            for f in range(6):
                n = nbr[f, e]
                w = (pat[f, e] * (n // count == me).astype(jnp.int32)).astype(F32)
                parts.append(src[lax.rem(n, count)] * jnp.full((basis, width), w, F32).astype(BF16))
            stacked = jnp.concatenate(parts, axis=0)
            acc[e] = jnp.dot(h_ref[e], stacked, preferred_element_type=F32)
            return carry

        lax.fori_loop(0, count, body, 0, unroll=4)

    def image(stage, e, layer):
        face = 0 if layer == 1 else 1
        side = 1 if layer == 1 else 0
        w = pat[face, e].astype(F32)
        block = halo[stage][side][lax.rem(nbr[face, e], LAYER)]
        block = block * jnp.full((basis, width), w, F32).astype(BF16)
        strip = h_ref[e, :, (1 + face) * basis:(2 + face) * basis]
        return acc[e] + jnp.dot(strip, block, preferred_element_type=F32)

    load_v.wait()
    first = exchange(0, v_ref)
    for c in first:
        c.start()
    load_h.wait()
    local_part(v_ref)
    second = exchange(1, f_ref)
    for layer in range(2):
        first[layer].wait_recv()

        def one(i, carry):
            e = layer * LAYER + i
            f_ref[e] = ((image(0, e, layer) - CENTER * v_ref[e].astype(F32)) / HALF_WIDTH).astype(BF16)
            return carry

        lax.fori_loop(0, LAYER, one, 0, unroll=4)
        second[1 - layer].start()
    local_part(f_ref)

    def swap(t, source):
        lanes = pl.ds(pl.multiple_of(source * width, width), width)
        return remote(
            y_ref.at[pl.ds(t * rows, rows)], z_ref.at[:, lanes],
            swap_send.at[t], swap_recv.at[source], {"state": t},
        )

    for layer in range(2):
        second[layer].wait_recv()

        def two(i, carry):
            e = layer * LAYER + i
            out = 2.0 * (image(1, e, layer) - CENTER * f_ref[e].astype(F32)) / HALF_WIDTH
            y_ref[pl.ds(pl.multiple_of(e * basis, basis), basis), :] = (out - v_ref[e].astype(F32)).astype(BF16)
            return carry

        lax.fori_loop(0, LAYER, two, 0, unroll=4)
        for t in range(layer * states // 2, (layer + 1) * states // 2):

            @pl.when(ms != t)
            def _():
                swap(t, ms).start()

    z_ref[:, pl.ds(pl.multiple_of(ms * width, width), width)] = y_ref[
        pl.ds(pl.multiple_of(ms * rows, rows), rows), :
    ]
    for c in first + second:
        c.wait_send()
    for t in range(states):

        @pl.when(ms != t)
        def _():
            swap(t, t).wait_recv()

    other = device(None, None, 1 - core)
    mine = pl.multiple_of(core * HALF, TILE)
    theirs = pl.multiple_of((1 - core) * HALF, TILE)

    def product(half, stream):
        at = half * HALF + STREAM_AT[stream]
        for i, j, n in runs((FIRST, SECOND)[stream][half]):
            strip = lax.dot_general(
                z_ref[:, i * BLK:(i + 1) * BLK], z_ref[:, j * BLK:(j + n) * BLK],
                (((0,), (0,)), ((), ())), preferred_element_type=F32,
            )
            for b in range(n):
                gram[at:at + BLK, :] = strip[:, b * BLK:(b + 1) * BLK]
                at += BLK

    def hand(stream):
        spot = pl.ds(STREAM_AT[stream], STREAM_ROWS[stream])
        return remote(
            gram.at[pl.ds(theirs + STREAM_AT[stream], STREAM_ROWS[stream])], pair.at[spot],
            core_send.at[stream], core_recv.at[stream], other,
        )

    for c in range(2):

        @pl.when(core == c)
        def _():
            for stream in range(2):
                product(1 - c, stream)
                hand(stream).start()
            for stream in range(2):
                product(c, stream)

    def ds(start, length):
        return pl.ds(pl.multiple_of(start, TILE), length)

    length_a = [STREAM_ROWS[s] // 8 for s in range(2)]
    length_b = [STREAM_ROWS[s] // 32 for s in range(2)]
    start_0 = [[mine + STREAM_AT[s] + p * STREAM_ROWS[s] // 2 for p in range(2)] for s in range(2)]
    start_a = [[start_0[s][p] + place[p] * length_a[s] for p in range(2)] for s in range(2)]
    start_b = [[start_a[s][p] + place[1 - p] * length_b[s] for p in range(2)] for s in range(2)]
    started = []

    def launch(copies):
        for c in copies:
            c.start()
        started.extend(copies)
        return copies

    def scatter(level, s):
        length = (length_a, length_b)[level][s]
        copies = []
        for d in range(1, 4):
            for p in range(2):
                dim = p if level == 0 else 1 - p
                to = peer(dim, d)
                start = (start_0, start_a)[level][s][p] + to * length
                copies.append(
                    remote(
                        gram.at[ds(start, length)], (buf_a, buf_b)[level].at[s, p, d, pl.ds(0, length)],
                        up_send.at[level, s, p, d], up_recv.at[level, s, p, d], device(dim, to, core),
                    )
                )
        return launch(copies)

    def gather_sums(level, s, copies):
        length = (length_a, length_b)[level][s]
        for c in copies:
            c.wait_recv()
        for p in range(2):
            own = ds((start_a, start_b)[level][s][p], length)
            total = gram[own, :]
            for d in range(1, 4):
                total = total + (buf_a, buf_b)[level][s, p, d, pl.ds(0, length), :]
            gram[own, :] = total

    def tile_of(s, z):
        return start_b[s][0] + (z // 4) * (start_b[s][1] - start_b[s][0]) + lax.rem(z, 4) * TILE

    def scatter_z(s):
        copies = []
        for d in range(1, 8):
            to = peer(2, d)
            copies.append(
                remote(
                    gram.at[ds(tile_of(s, to), TILE)], buf_c.at[s, d],
                    up_send.at[2, s, 0, d], up_recv.at[2, s, 0, d], device(2, to, core),
                )
            )
        if s == 1:
            for p in range(2):
                spare = ds(start_b[1][p] + 4 * TILE, TILE)
                buf_d[place[2], p] = gram[spare, :]
            for d in range(1, 8):
                copies.append(
                    remote(
                        buf_d.at[place[2]], buf_d.at[place[2]],
                        up_send.at[2, s, 1, d], up_recv.at[2, s, 1, d], device(2, peer(2, d), core),
                    )
                )
        return launch(copies)

    def finish_z(s, copies):
        for c in copies:
            c.wait_recv()
        own = ds(tile_of(s, place[2]), TILE)
        total = gram[own, :]
        for d in range(1, 8):
            total = total + buf_c[s, d]
        res[own, :] = total
        if s == 1:
            for p in range(2):
                total = buf_d[0, p]
                for z in range(1, 8):
                    total = total + buf_d[z, p]
                res[ds(start_b[1][p] + 4 * TILE, TILE), :] = total

    def spread_z(s):
        own = ds(tile_of(s, place[2]), TILE)
        return launch([
            remote(
                res.at[own], res.at[own], down_send.at[2, s, 0, d], down_recv.at[2, s, 0, d],
                device(2, peer(2, d), core),
            )
            for d in range(1, 8)
        ])

    def spread(level, s):
        copies = []
        for d in range(1, 4):
            for p in range(2):
                dim = p if level == 0 else 1 - p
                own = ds((start_a, start_b)[level][s][p], (length_a, length_b)[level][s])
                copies.append(
                    remote(
                        res.at[own], res.at[own], down_send.at[level, s, p, d], down_recv.at[level, s, p, d],
                        device(dim, peer(dim, d), core),
                    )
                )
        return launch(copies)

    def arrived(copies):
        for c in copies:
            c.wait_recv()

    def give(s):
        own = ds(mine + STREAM_AT[s], STREAM_ROWS[s])
        return launch([remote(res.at[own], res.at[own], core_send.at[2 + s], core_recv.at[2 + s], other)])

    stage = [None, None]
    for s in range(2):
        hand(s).wait_recv()
        own = ds(mine + STREAM_AT[s], STREAM_ROWS[s])
        gram[own, :] = gram[own, :] + pair[pl.ds(STREAM_AT[s], STREAM_ROWS[s]), :]
        stage[s] = scatter(0, s)
    for s in range(2):
        gather_sums(0, s, stage[s])
        stage[s] = scatter(1, s)
        if s == 0:
            gather_sums(1, s, stage[s])
            stage[s] = scatter_z(s)
    gather_sums(1, 1, stage[1])
    stage[1] = scatter_z(1)
    for s in range(2):
        finish_z(s, stage[s])
        stage[s] = spread_z(s)
    for s in range(2):
        arrived(stage[s])
        stage[s] = spread(1, s)
    for s in range(2):
        arrived(stage[s])
        stage[s] = spread(0, s)
    arrived(stage[0])
    stage[0] = give(0)

    blocks = states * width // BLK
    at = [pl.ds(k * BLK, BLK) for k in range(blocks)]
    early = set(FIRST[0] + FIRST[1])
    own_rows = pl.ds(pl.multiple_of(ms * rows, rows), rows)

    def unpack(wanted):
        for spot, (i, j) in enumerate(packed_blocks()):
            if ((i, j) in early) == wanted:
                mat[at[i], at[j]] = res[spot * BLK:(spot + 1) * BLK, :] * scale

    def hand_over(t):
        return remote(out.at[t], o_ref.at[own_rows], send.at[t], recv.at[ms], {"state": t})

    def rotate_block(t):
        strip = mat[at[t], :(t + 1) * BLK].astype(BF16)
        block = lax.dot_general(
            z_ref[:, :(t + 1) * BLK], strip, (((1,), (1,)), ((), ())), preferred_element_type=F32
        ).astype(BF16)

        @pl.when(ms == t)
        def _():
            o_ref[own_rows, :] = block

        @pl.when(ms != t)
        def _():
            out[t] = block
            hand_over(t).start()

    def apply(k, i, diagonal, known=False):
        slot = k % 2
        if diagonal:
            mat[at[i], at[i]] = mat[at[i], at[i]] - sdot(left_terms[slot, :, at[i]], right_terms[slot, :, at[i]])
            return
        lhs = left_terms[slot, :, at[i]]
        old = pl.ds(0, (k + 1) * BLK)
        change = sdot(lhs, right_terms[slot, :, old])
        if k > 0:
            done = pl.ds(0, k * BLK)
            mat[at[i], done] = mat[at[i], done] - change[:, :k * BLK]
        mat[at[i], at[k]] = -change[:, k * BLK:]
        first = i + 1 if known else i
        if first < blocks:
            new = pl.ds(first * BLK, (blocks - first) * BLK)
            mat[at[i], new] = mat[at[i], new] - sdot(lhs, right_terms[slot, :, new])

    for k in range(blocks):
        if k == 0:
            arrived(stage[0])
            unpack(True)
        if k == 1:
            arrived(stage[1])
            stage[1] = give(1)
        if k == 2:
            arrived(stage[1])
            unpack(False)
        todo = [[(k - 1, i, i == k)] for i in range(k, blocks)]
        if k == 0:
            todo = []
        elif k == 1:
            todo = todo[:1]
        elif k == 2:
            todo = [[(0, i, i == 2), (1, i, i == 2)] for i in range(2, blocks)]

        def aside(p, todo=todo):
            for group in todo[p::BLK // BASE]:
                for source, i, known in group:
                    apply(source, i, False, known)

        corner = factor_block(mat[at[k], at[k]], aside)
        mat[at[k], at[k]] = corner
        lhs = left_stack(corner.T)
        slot = k % 2
        pieces = []
        if k > 0:
            done = pl.ds(0, k * BLK)
            pieces.append((done, sdot(lhs, right_stack(mat[at[k], done]))))
        if k + 1 < blocks:
            new = pl.ds((k + 1) * BLK, (blocks - k - 1) * BLK)
            pieces.append((new, sdot(lhs, right_stack(mat[at[k], new]))))
            right_terms[slot, :, at[k]] = right_stack(corner)
        for where, piece in pieces:
            mat[at[k], where] = piece
            if k + 1 < blocks:
                right_terms[slot, :, where] = right_stack(piece)
        if k + 1 < blocks:
            left_terms[slot, :, new] = left_stack(pieces[-1][1])
            apply(k, k + 1, True)
        if k == 0:
            apply(0, 2, True)
        rotate_block(k)
    for t in range(states):

        @pl.when(ms != t)
        def _():
            hand_over(t).wait_send()
            rows_of = o_ref.at[pl.ds(t * rows, rows)]
            remote(out.at[t], rows_of, send.at[t], recv.at[t], {"state": t}).wait_recv()
    for c in started:
        c.wait_send()
    for s in range(2):
        hand(s).wait_send()
    for t in range(states):

        @pl.when(ms != t)
        def _():
            swap(t, ms).wait_send()


def whole(coefficients, hamiltonian, neighbours, pattern, elems, states):
    count, basis, width = coefficients.shape
    rows = count * basis // states
    n = states * width
    scale = 1.0 / (count * elems * basis)
    dma = pltpu.SemaphoreType.DMA
    return pl.pallas_call(
        functools.partial(whole_kernel, elems, states, scale),
        out_shape=jax.ShapeDtypeStruct((count * basis, width), BF16),
        in_specs=[in_smem(), in_smem(), in_hbm(), in_hbm()],
        out_specs=in_vmem(),
        scratch_shapes=[
            VMEM((rows, n), BF16),
            VMEM((2 * HALF, BLK), F32),
            VMEM((n, n), F32),
            VMEM((2, 6 * BLK, n), BF16),
            VMEM((2, 6 * BLK, n), BF16),
            VMEM((states, rows, width), BF16),
            dma((states,)),
            dma((states,)),
            VMEM(coefficients.shape, BF16),
            VMEM(hamiltonian.shape, BF16),
            dma((2,)),
            VMEM((count, basis, width), F32),
            VMEM((count, basis, width), BF16),
            VMEM((count * basis, width), BF16),
            VMEM((LAYER, basis, width), BF16),
            VMEM((LAYER, basis, width), BF16),
            VMEM((LAYER, basis, width), BF16),
            VMEM((LAYER, basis, width), BF16),
            dma((2, 2)),
            dma((2, 2)),
            dma((states,)),
            dma((states,)),
            VMEM((2 * HALF, BLK), F32),
            VMEM((HALF, BLK), F32),
            VMEM((2, 2, 4, WIDE, BLK), F32),
            VMEM((2, 2, 4, WIDE // 4, BLK), F32),
            VMEM((2, 8, TILE, BLK), F32),
            VMEM((8, 2, TILE, BLK), F32),
            dma((4,)),
            dma((4,)),
            dma((3, 2, 2, 8)),
            dma((3, 2, 2, 8)),
            dma((3, 2, 2, 8)),
            dma((3, 2, 2, 8)),
        ],
        compiler_params=pltpu.CompilerParams(
            collective_id=0, has_side_effects=True, vmem_limit_bytes=60 * MIB
        ),
        cost_estimate=pl.CostEstimate(flops=12 * 10**9, bytes_accessed=8 * MIB, transcendentals=0),
    )(neighbours.T, pattern.T, coefficients, hamiltonian)


def on_device(coefficients, hamiltonian, neighbours, pattern):
    count, basis, width = coefficients.shape
    elems = lax.axis_size("elem")
    states = lax.axis_size("state")
    result = whole(coefficients, hamiltonian, neighbours, pattern, elems, states)
    return result.reshape(count, basis, width)


def solution(mesh):
    return jax.shard_map(
        on_device,
        mesh=mesh,
        in_specs=(
            P("elem", None, "state"),
            P("elem", None, None),
            P("elem", None),
            P("elem", None),
        ),
        out_specs=P("elem", None, "state"),
        check_vma=False,
    )
```

```python
import functools

import jax
import jax.numpy as jnp
from jax import lax
from jax.experimental import pallas as pl
from jax.experimental.pallas import tpu as pltpu
from jax.sharding import PartitionSpec as P

LAYER = 32
CENTER = 0.5
HALF_WIDTH = 2.0
BLK = 128
BASE = 32
F32 = jnp.float32
BF16 = jnp.bfloat16
MESH = pl.DeviceIdType.MESH
VMEM = pltpu.VMEM
MIB = 1024 * 1024


def in_vmem():
    return pl.BlockSpec(memory_space=pltpu.VMEM)


def in_hbm():
    return pl.BlockSpec(memory_space=pl.ANY)


def in_smem():
    return pl.BlockSpec(memory_space=pltpu.SMEM)


def greet(devices):
    barrier = pltpu.get_barrier_semaphore()
    for device in devices:
        pl.semaphore_signal(barrier, inc=1, device_id=device, device_id_type=MESH)
    pl.semaphore_wait(barrier, len(devices))


def remote(src, dst, send, recv, device):
    return pltpu.make_async_remote_copy(
        src_ref=src, dst_ref=dst, send_sem=send, recv_sem=recv, device_id=device, device_id_type=MESH
    )


def recip(x):
    q = pl.reciprocal(x, approx=True)
    return q * (2.0 - x * q)


def split(x):
    h = x.astype(BF16)
    r = x - h.astype(F32)
    m = r.astype(BF16)
    return h, m, (r - m.astype(F32)).astype(BF16)


def left_stack(x):
    h, m, l = split(x)
    return jnp.concatenate([h, h, m, h, m, l], axis=0)


def right_stack(x):
    h, m, l = split(x)
    return jnp.concatenate([h, m, h, l, m, h], axis=0)


def sdot(a, b):
    return lax.dot_general(a, b, (((0,), (0,)), ((), ())), preferred_element_type=F32)


def base_step(p, panel):
    r0 = p * BASE
    lane = lax.broadcasted_iota(jnp.int32, (8, BLK), 1)
    sub = lax.broadcasted_iota(jnp.int32, (8, BLK), 0)
    groups = BASE // 8
    rows = [panel[8 * g:8 * g + 8] for g in range(groups)]
    cols = [
        {g: jnp.broadcast_to(rows[g][:, r0 + k:r0 + k + 1], (8, BLK)) for g in range(k // 8, groups)}
        for k in range(BASE)
    ]
    inside = (lane >= r0) & (lane < r0 + BASE)
    rows = [
        jnp.where(inside, (lane - r0 == sub + 8 * g).astype(F32), rows[g]) for g in range(groups)
    ]
    scales = [jnp.ones((8, BLK), F32) for _ in range(groups)]

    def at(vecs, i):
        return jnp.broadcast_to(vecs[i // 8][i % 8:i % 8 + 1], (8, BLK))

    for j in range(0, BASE, 2):
        gj, sj = divmod(j, 8)
        a, b, d = at(cols[j], j), at(cols[j], j + 1), at(cols[j + 1], j + 1)
        det = a * d - b * b
        ra = recip(a)
        rdet = recip(det)
        slope = b * ra
        inv = a * rdet
        scales[gj] = jnp.where(sub == sj, a, jnp.where(sub == sj + 1, det * ra, scales[gj]))
        first, reduced, second = {}, {}, {}
        for g in range(gj, groups):
            c = cols[j][g]
            first[g] = c * ra
            reduced[g] = cols[j + 1][g] - c * slope
            second[g] = reduced[g] * inv
            if g == gj:
                first[g] = jnp.where(sub > sj + 1, first[g], 0.0)
                second[g] = jnp.where(sub > sj + 1, second[g], 0.0)
        for k in range(j + 2, BASE):
            low, high = at(cols[j], k), at(reduced, k)
            for g in range(k // 8, groups):
                cols[k][g] = cols[k][g] - first[g] * low - second[g] * high
        low = at(rows, j)
        high = at(rows, j + 1) - slope * low
        rows[gj] = jnp.where(sub == sj + 1, high, rows[gj])
        for g in range(gj, groups):
            if 8 * g + 7 > j + 1:
                rows[g] = rows[g] - first[g] * low - second[g] * high
    return jnp.concatenate([rows[g] * lax.rsqrt(scales[g]) for g in range(groups)], axis=0)


def factor_block(block, aside):
    rr = lax.broadcasted_iota(jnp.int32, (BLK, BLK), 0)
    cc = lax.broadcasted_iota(jnp.int32, (BLK, BLK), 1)
    diagonal = jnp.where(rr == cc, block, 0.0)
    across = lax.rsqrt(jnp.sum(diagonal, axis=0, keepdims=True))
    down = lax.rsqrt(jnp.sum(diagonal, axis=1, keepdims=True))
    rest = block * across * down
    parts = []
    for p in range(BLK // BASE):
        aside(p)
        done = base_step(p, rest[:BASE])
        parts.append(done)
        if p + 1 < BLK // BASE:
            r1 = (p + 1) * BASE
            lane = lax.broadcasted_iota(jnp.int32, (BLK - r1, BLK), 1)
            update = sdot(left_stack(done)[:, r1:], right_stack(done))
            rest = jnp.where((lane >= r1 - BASE) & (lane < r1), 0.0, rest[BASE:]) - update
    return jnp.where(cc <= rr, jnp.concatenate(parts, axis=0), 0.0) * across


FIRST = (
    [(0, j) for j in range(8)],
    [(1, j) for j in range(1, 8)] + [(2, 2)],
)
SECOND = (
    [(2, j) for j in range(3, 8)] + [(3, j) for j in range(3, 8)],
    [(i, j) for i in range(4, 8) for j in range(i, 8)],
)
HALF = (len(FIRST[0]) + len(SECOND[0])) * BLK
STREAM_ROWS = (len(FIRST[0]) * BLK, len(SECOND[0]) * BLK)
STREAM_AT = (0, STREAM_ROWS[0])
SIZES = (4, 4, 8)
TILE = 8
WIDE = STREAM_ROWS[1] // 8


def packed_blocks():
    return FIRST[0] + SECOND[0] + FIRST[1] + SECOND[1]


def runs(pairs):
    found = []
    for i, j in pairs:
        if found and found[-1][0] == i and found[-1][1] + found[-1][2] == j:
            found[-1][2] += 1
        else:
            found.append([i, j, 1])
    return found


def whole_kernel(
    elems, states, scale, nbr, pat, v_hbm, h_hbm, o_ref,
    z_ref, res, mat, left_terms, right_terms, out, send, recv,
    v_ref, h_ref, load, acc, f_ref, y_ref, tail_a, head_a, tail_b, head_b,
    halo_send, halo_recv, swap_send, swap_recv,
    gram, pair, buf_a, buf_b, buf_c, buf_d,
    core_send, core_recv, up_send, up_recv, down_send, down_recv,
):
    count, basis, width = v_ref.shape
    rows = count * basis // states
    per = count // states
    me = lax.axis_index("elem")
    ms = lax.axis_index("state")
    right = lax.rem(me + 1, elems)
    left = lax.rem(me + elems - 1, elems)
    core = lax.rem(me, 2)
    place = [lax.rem(ms, 4), (ms // 4) * 2 + me // 16, lax.rem(me, 16) // 2]

    def device(dim, at, c):
        spot = list(place)
        if dim is not None:
            spot[dim] = at
        x, y, z = spot
        return {"elem": lax.rem(y, 2) * 16 + z * 2 + c, "state": (y // 2) * 4 + x}

    def peer(dim, d):
        return lax.rem(place[dim] + d, SIZES[dim])

    load_v = pltpu.make_async_copy(v_hbm, v_ref, load.at[0])
    load_h = pltpu.make_async_copy(h_hbm, h_ref, load.at[1])
    load_v.start()
    load_h.start()
    greet(
        [{"elem": right}, {"elem": left}]
        + [{"state": lax.rem(ms + d, states)} for d in range(1, states)]
        + [device(1, peer(1, d), core) for d in (1, 3)]
        + [device(2, peer(2, d), core) for d in range(1, 8)]
    )

    halo = ((tail_a, head_a), (tail_b, head_b))

    def exchange(stage, src):
        tail = remote(
            src.at[pl.ds(count - LAYER, LAYER)], halo[stage][0],
            halo_send.at[stage, 0], halo_recv.at[stage, 0], {"elem": right},
        )
        head = remote(
            src.at[pl.ds(0, LAYER)], halo[stage][1],
            halo_send.at[stage, 1], halo_recv.at[stage, 1], {"elem": left},
        )
        return tail, head

    def local_part(src):
        def body(e, carry):
            parts = [src[e]]
            for f in range(6):
                n = nbr[f, e]
                w = (pat[f, e] * (n // count == me).astype(jnp.int32)).astype(F32)
                parts.append(src[lax.rem(n, count)] * jnp.full((basis, width), w, F32).astype(BF16))
            stacked = jnp.concatenate(parts, axis=0)
            acc[e] = jnp.dot(h_ref[e], stacked, preferred_element_type=F32)
            return carry

        lax.fori_loop(0, count, body, 0, unroll=4)

    def image(stage, e, layer):
        face = 0 if layer == 1 else 1
        side = 1 if layer == 1 else 0
        w = pat[face, e].astype(F32)
        block = halo[stage][side][lax.rem(nbr[face, e], LAYER)]
        block = block * jnp.full((basis, width), w, F32).astype(BF16)
        strip = h_ref[e, :, (1 + face) * basis:(2 + face) * basis]
        return acc[e] + jnp.dot(strip, block, preferred_element_type=F32)

    load_v.wait()
    first = exchange(0, v_ref)
    for c in first:
        c.start()
    load_h.wait()
    local_part(v_ref)
    second = exchange(1, f_ref)
    def stage_one(layer):
        first[layer].wait_recv()

        def one(i, carry):
            e = layer * LAYER + i
            f_ref[e] = ((image(0, e, layer) - CENTER * v_ref[e].astype(F32)) / HALF_WIDTH).astype(BF16)
            return carry

        lax.fori_loop(0, LAYER, one, 0, unroll=4)
        second[1 - layer].start()

    for c in range(2):

        @pl.when(core == c)
        def _():
            stage_one(1 - c)
            stage_one(c)

    local_part(f_ref)

    def swap(t, source):
        lanes = pl.ds(pl.multiple_of(source * width, width), width)
        return remote(
            y_ref.at[pl.ds(t * rows, rows)], z_ref.at[:, lanes],
            swap_send.at[t], swap_recv.at[source], {"state": t},
        )

    def stage_two(layer):
        second[layer].wait_recv()

        def two(i, carry):
            e = layer * LAYER + i
            out = 2.0 * (image(1, e, layer) - CENTER * f_ref[e].astype(F32)) / HALF_WIDTH
            y_ref[pl.ds(pl.multiple_of(e * basis, basis), basis), :] = (out - v_ref[e].astype(F32)).astype(BF16)
            return carry

        lax.fori_loop(0, LAYER, two, 0, unroll=4)
        for t in range(layer * states // 2, (layer + 1) * states // 2):

            @pl.when(ms != t)
            def _():
                swap(t, ms).start()

    for c in range(2):

        @pl.when(core == c)
        def _():
            stage_two(1 - c)
            stage_two(c)

    z_ref[:, pl.ds(pl.multiple_of(ms * width, width), width)] = y_ref[
        pl.ds(pl.multiple_of(ms * rows, rows), rows), :
    ]
    for c in first + second:
        c.wait_send()
    for t in range(states):

        @pl.when(ms != t)
        def _():
            swap(t, t).wait_recv()

    other = device(None, None, 1 - core)
    mine = pl.multiple_of(core * HALF, TILE)
    theirs = pl.multiple_of((1 - core) * HALF, TILE)

    def product(half, stream):
        at = half * HALF + STREAM_AT[stream]
        for i, j, n in runs((FIRST, SECOND)[stream][half]):
            strip = lax.dot_general(
                z_ref[:, i * BLK:(i + 1) * BLK], z_ref[:, j * BLK:(j + n) * BLK],
                (((0,), (0,)), ((), ())), preferred_element_type=F32,
            )
            for b in range(n):
                gram[at:at + BLK, :] = strip[:, b * BLK:(b + 1) * BLK]
                at += BLK

    def hand(stream):
        spot = pl.ds(STREAM_AT[stream], STREAM_ROWS[stream])
        return remote(
            gram.at[pl.ds(theirs + STREAM_AT[stream], STREAM_ROWS[stream])], pair.at[spot],
            core_send.at[stream], core_recv.at[stream], other,
        )

    for c in range(2):

        @pl.when(core == c)
        def _():
            for stream in range(2):
                product(1 - c, stream)
                hand(stream).start()
            for stream in range(2):
                product(c, stream)

    def ds(start, length):
        return pl.ds(pl.multiple_of(start, TILE), length)

    length_a = [STREAM_ROWS[s] // 8 for s in range(2)]
    length_b = [STREAM_ROWS[s] // 32 for s in range(2)]
    start_0 = [[mine + STREAM_AT[s] + p * STREAM_ROWS[s] // 2 for p in range(2)] for s in range(2)]
    start_a = [[start_0[s][p] + place[p] * length_a[s] for p in range(2)] for s in range(2)]
    start_b = [[start_a[s][p] + place[1 - p] * length_b[s] for p in range(2)] for s in range(2)]
    started = []

    def launch(copies):
        for c in copies:
            c.start()
        started.extend(copies)
        return copies

    def scatter(level, s):
        length = (length_a, length_b)[level][s]
        copies = []
        for d in range(1, 4):
            for p in range(2):
                dim = p if level == 0 else 1 - p
                to = peer(dim, d)
                start = (start_0, start_a)[level][s][p] + to * length
                copies.append(
                    remote(
                        gram.at[ds(start, length)], (buf_a, buf_b)[level].at[s, p, d, pl.ds(0, length)],
                        up_send.at[level, s, p, d], up_recv.at[level, s, p, d], device(dim, to, core),
                    )
                )
        return launch(copies)

    def gather_sums(level, s, copies):
        length = (length_a, length_b)[level][s]
        for c in copies:
            c.wait_recv()
        for p in range(2):
            own = ds((start_a, start_b)[level][s][p], length)
            total = gram[own, :]
            for d in range(1, 4):
                total = total + (buf_a, buf_b)[level][s, p, d, pl.ds(0, length), :]
            gram[own, :] = total

    def tile_of(s, z):
        return start_b[s][0] + (z // 4) * (start_b[s][1] - start_b[s][0]) + lax.rem(z, 4) * TILE

    def scatter_z(s):
        copies = []
        for d in range(1, 8):
            to = peer(2, d)
            copies.append(
                remote(
                    gram.at[ds(tile_of(s, to), TILE)], buf_c.at[s, d],
                    up_send.at[2, s, 0, d], up_recv.at[2, s, 0, d], device(2, to, core),
                )
            )
        if s == 1:
            for p in range(2):
                spare = ds(start_b[1][p] + 4 * TILE, TILE)
                buf_d[place[2], p] = gram[spare, :]
            for d in range(1, 8):
                copies.append(
                    remote(
                        buf_d.at[place[2]], buf_d.at[place[2]],
                        up_send.at[2, s, 1, d], up_recv.at[2, s, 1, d], device(2, peer(2, d), core),
                    )
                )
        return launch(copies)

    def finish_z(s, copies):
        for c in copies:
            c.wait_recv()
        own = ds(tile_of(s, place[2]), TILE)
        total = gram[own, :]
        for d in range(1, 8):
            total = total + buf_c[s, d]
        res[own, :] = total
        if s == 1:
            for p in range(2):
                total = buf_d[0, p]
                for z in range(1, 8):
                    total = total + buf_d[z, p]
                res[ds(start_b[1][p] + 4 * TILE, TILE), :] = total

    def spread_z(s):
        own = ds(tile_of(s, place[2]), TILE)
        return launch([
            remote(
                res.at[own], res.at[own], down_send.at[2, s, 0, d], down_recv.at[2, s, 0, d],
                device(2, peer(2, d), core),
            )
            for d in range(1, 8)
        ])

    def spread(level, s):
        copies = []
        for d in range(1, 4):
            for p in range(2):
                dim = p if level == 0 else 1 - p
                own = ds((start_a, start_b)[level][s][p], (length_a, length_b)[level][s])
                copies.append(
                    remote(
                        res.at[own], res.at[own], down_send.at[level, s, p, d], down_recv.at[level, s, p, d],
                        device(dim, peer(dim, d), core),
                    )
                )
        return launch(copies)

    def arrived(copies):
        for c in copies:
            c.wait_recv()

    def give(s):
        own = ds(mine + STREAM_AT[s], STREAM_ROWS[s])
        return launch([remote(res.at[own], res.at[own], core_send.at[2 + s], core_recv.at[2 + s], other)])

    stage = [None, None]
    for s in range(2):
        hand(s).wait_recv()
        own = ds(mine + STREAM_AT[s], STREAM_ROWS[s])
        gram[own, :] = gram[own, :] + pair[pl.ds(STREAM_AT[s], STREAM_ROWS[s]), :]
        stage[s] = scatter(0, s)
    for s in range(2):
        gather_sums(0, s, stage[s])
        stage[s] = scatter(1, s)
        if s == 0:
            gather_sums(1, s, stage[s])
            stage[s] = scatter_z(s)
    gather_sums(1, 1, stage[1])
    stage[1] = scatter_z(1)
    for s in range(2):
        finish_z(s, stage[s])
        stage[s] = spread_z(s)
    for s in range(2):
        arrived(stage[s])
        stage[s] = spread(1, s)
    for s in range(2):
        arrived(stage[s])
        stage[s] = spread(0, s)
    arrived(stage[0])
    stage[0] = give(0)

    blocks = states * width // BLK
    at = [pl.ds(k * BLK, BLK) for k in range(blocks)]
    early = set(FIRST[0] + FIRST[1])
    own_rows = pl.ds(pl.multiple_of(ms * rows, rows), rows)

    def unpack(wanted):
        for spot, (i, j) in enumerate(packed_blocks()):
            if ((i, j) in early) == wanted:
                mat[at[i], at[j]] = res[spot * BLK:(spot + 1) * BLK, :] * scale

    def hand_over(t):
        return remote(out.at[t], o_ref.at[own_rows], send.at[t], recv.at[ms], {"state": t})

    def rotate_block(t):
        strip = mat[at[t], :(t + 1) * BLK].astype(BF16)
        out[t] = lax.dot_general(
            z_ref[:, :(t + 1) * BLK], strip, (((1,), (1,)), ((), ())), preferred_element_type=F32
        ).astype(BF16)

    def send_block(t):
        @pl.when(ms == t)
        def _():
            o_ref[own_rows, :] = out[t]

        @pl.when(ms != t)
        def _():
            hand_over(t).start()

    def rest_of_panel(k):
        slot = k % 2
        lhs = left_stack(mat[at[k], at[k]].T)
        places = [pl.ds(0, k * BLK)] if k > 0 else []
        if k + 2 < blocks:
            places.append(pl.ds((k + 2) * BLK, (blocks - k - 2) * BLK))
        for where in places:
            piece = sdot(lhs, right_stack(mat[at[k], where]))
            mat[at[k], where] = piece
            if k + 1 < blocks:
                right_terms[slot, :, where] = right_stack(piece)
        if k + 1 < blocks:
            right_terms[slot, :, at[k]] = right_stack(mat[at[k], at[k]])
        if k + 2 < blocks:
            left_terms[slot, :, where] = left_stack(piece)

    def apply(k, i, diagonal, known=False):
        slot = k % 2
        if diagonal:
            mat[at[i], at[i]] = mat[at[i], at[i]] - sdot(left_terms[slot, :, at[i]], right_terms[slot, :, at[i]])
            return
        lhs = left_terms[slot, :, at[i]]
        old = pl.ds(0, (k + 1) * BLK)
        change = sdot(lhs, right_terms[slot, :, old])
        if k > 0:
            done = pl.ds(0, k * BLK)
            mat[at[i], done] = mat[at[i], done] - change[:, :k * BLK]
        mat[at[i], at[k]] = -change[:, k * BLK:]
        first = i + 1 if known else i
        if first < blocks:
            new = pl.ds(first * BLK, (blocks - first) * BLK)
            mat[at[i], new] = mat[at[i], new] - sdot(lhs, right_terms[slot, :, new])

    for k in range(blocks):
        if k == 0:
            arrived(stage[0])
            unpack(True)
        if k == 1:
            arrived(stage[1])
            stage[1] = give(1)
        if k == 2:
            arrived(stage[1])
            unpack(False)
        todo = [[(k - 1, i, i == k)] for i in range(k, blocks)]
        if k == 0:
            todo = []
        elif k == 1:
            todo = todo[:1]
        elif k == 2:
            todo = [[(0, i, i == 2), (1, i, i == 2)] for i in range(2, blocks)]

        def aside(p, k=k, todo=todo):
            if p == 0 and k > 0:
                rest_of_panel(k - 1)
                return
            if p == 1 and k > 0:
                rotate_block(k - 1)
            if p == 2 and k == 1:
                apply(0, 2, True)
            for group in todo[max(p - 1, 0)::BLK // BASE - 1]:
                for source, i, known in group:
                    apply(source, i, False, known)

        corner = factor_block(mat[at[k], at[k]], aside)
        mat[at[k], at[k]] = corner
        if k > 0:
            send_block(k - 1)
        if k + 1 < blocks:
            slot = k % 2
            piece = sdot(left_stack(corner.T), right_stack(mat[at[k], at[k + 1]]))
            mat[at[k], at[k + 1]] = piece
            right_terms[slot, :, at[k + 1]] = right_stack(piece)
            left_terms[slot, :, at[k + 1]] = left_stack(piece)
            apply(k, k + 1, True)
        else:
            rest_of_panel(k)
            rotate_block(k)
            send_block(k)
    for t in range(states):

        @pl.when(ms != t)
        def _():
            hand_over(t).wait_send()
            rows_of = o_ref.at[pl.ds(t * rows, rows)]
            remote(out.at[t], rows_of, send.at[t], recv.at[t], {"state": t}).wait_recv()
    for c in started:
        c.wait_send()
    for s in range(2):
        hand(s).wait_send()
    for t in range(states):

        @pl.when(ms != t)
        def _():
            swap(t, ms).wait_send()


def whole(coefficients, hamiltonian, neighbours, pattern, elems, states):
    count, basis, width = coefficients.shape
    rows = count * basis // states
    n = states * width
    scale = 1.0 / (count * elems * basis)
    dma = pltpu.SemaphoreType.DMA
    return pl.pallas_call(
        functools.partial(whole_kernel, elems, states, scale),
        out_shape=jax.ShapeDtypeStruct((count * basis, width), BF16),
        in_specs=[in_smem(), in_smem(), in_hbm(), in_hbm()],
        out_specs=in_vmem(),
        scratch_shapes=[
            VMEM((rows, n), BF16),
            VMEM((2 * HALF, BLK), F32),
            VMEM((n, n), F32),
            VMEM((2, 6 * BLK, n), BF16),
            VMEM((2, 6 * BLK, n), BF16),
            VMEM((states, rows, width), BF16),
            dma((states,)),
            dma((states,)),
            VMEM(coefficients.shape, BF16),
            VMEM(hamiltonian.shape, BF16),
            dma((2,)),
            VMEM((count, basis, width), F32),
            VMEM((count, basis, width), BF16),
            VMEM((count * basis, width), BF16),
            VMEM((LAYER, basis, width), BF16),
            VMEM((LAYER, basis, width), BF16),
            VMEM((LAYER, basis, width), BF16),
            VMEM((LAYER, basis, width), BF16),
            dma((2, 2)),
            dma((2, 2)),
            dma((states,)),
            dma((states,)),
            VMEM((2 * HALF, BLK), F32),
            VMEM((HALF, BLK), F32),
            VMEM((2, 2, 4, WIDE, BLK), F32),
            VMEM((2, 2, 4, WIDE // 4, BLK), F32),
            VMEM((2, 8, TILE, BLK), F32),
            VMEM((8, 2, TILE, BLK), F32),
            dma((4,)),
            dma((4,)),
            dma((3, 2, 2, 8)),
            dma((3, 2, 2, 8)),
            dma((3, 2, 2, 8)),
            dma((3, 2, 2, 8)),
        ],
        compiler_params=pltpu.CompilerParams(
            collective_id=0, has_side_effects=True, vmem_limit_bytes=60 * MIB
        ),
        cost_estimate=pl.CostEstimate(flops=12 * 10**9, bytes_accessed=8 * MIB, transcendentals=0),
    )(neighbours.T, pattern.T, coefficients, hamiltonian)


def on_device(coefficients, hamiltonian, neighbours, pattern):
    count, basis, width = coefficients.shape
    elems = lax.axis_size("elem")
    states = lax.axis_size("state")
    result = whole(coefficients, hamiltonian, neighbours, pattern, elems, states)
    return result.reshape(count, basis, width)


def solution(mesh):
    return jax.shard_map(
        on_device,
        mesh=mesh,
        in_specs=(
            P("elem", None, "state"),
            P("elem", None, None),
            P("elem", None),
            P("elem", None),
        ),
        out_specs=P("elem", None, "state"),
        check_vma=False,
    )
```

```python
import functools

import jax
import jax.numpy as jnp
from jax import lax
from jax.experimental import pallas as pl
from jax.experimental.pallas import tpu as pltpu
from jax.sharding import PartitionSpec as P

LAYER = 32
CENTER = 0.5
HALF_WIDTH = 2.0
BLK = 128
BASE = 32
F32 = jnp.float32
BF16 = jnp.bfloat16
MESH = pl.DeviceIdType.MESH
VMEM = pltpu.VMEM
MIB = 1024 * 1024


def in_vmem():
    return pl.BlockSpec(memory_space=pltpu.VMEM)


def in_hbm():
    return pl.BlockSpec(memory_space=pl.ANY)


def in_smem():
    return pl.BlockSpec(memory_space=pltpu.SMEM)


def greet(devices):
    barrier = pltpu.get_barrier_semaphore()
    for device in devices:
        pl.semaphore_signal(barrier, inc=1, device_id=device, device_id_type=MESH)
    pl.semaphore_wait(barrier, len(devices))


def remote(src, dst, send, recv, device):
    return pltpu.make_async_remote_copy(
        src_ref=src, dst_ref=dst, send_sem=send, recv_sem=recv, device_id=device, device_id_type=MESH
    )


def recip(x):
    q = pl.reciprocal(x, approx=True)
    return q * (2.0 - x * q)


def split(x):
    h = x.astype(BF16)
    r = x - h.astype(F32)
    m = r.astype(BF16)
    return h, m, (r - m.astype(F32)).astype(BF16)


def left_stack(x):
    h, m, l = split(x)
    return jnp.concatenate([h, h, m, h, m, l], axis=0)


def right_stack(x):
    h, m, l = split(x)
    return jnp.concatenate([h, m, h, l, m, h], axis=0)


def sdot(a, b):
    return lax.dot_general(a, b, (((0,), (0,)), ((), ())), preferred_element_type=F32)


def base_step(p, panel):
    r0 = p * BASE
    lane = lax.broadcasted_iota(jnp.int32, (8, BLK), 1)
    sub = lax.broadcasted_iota(jnp.int32, (8, BLK), 0)
    groups = BASE // 8
    rows = [panel[8 * g:8 * g + 8] for g in range(groups)]
    cols = [
        {g: jnp.broadcast_to(rows[g][:, r0 + k:r0 + k + 1], (8, BLK)) for g in range(k // 8, groups)}
        for k in range(BASE)
    ]
    inside = (lane >= r0) & (lane < r0 + BASE)
    rows = [
        jnp.where(inside, (lane - r0 == sub + 8 * g).astype(F32), rows[g]) for g in range(groups)
    ]
    scales = [jnp.ones((8, BLK), F32) for _ in range(groups)]

    def at(vecs, i):
        return jnp.broadcast_to(vecs[i // 8][i % 8:i % 8 + 1], (8, BLK))

    for j in range(0, BASE, 2):
        gj, sj = divmod(j, 8)
        a, b, d = at(cols[j], j), at(cols[j], j + 1), at(cols[j + 1], j + 1)
        det = a * d - b * b
        ra = recip(a)
        rdet = recip(det)
        slope = b * ra
        inv = a * rdet
        scales[gj] = jnp.where(sub == sj, a, jnp.where(sub == sj + 1, det * ra, scales[gj]))
        first, reduced, second = {}, {}, {}
        for g in range(gj, groups):
            c = cols[j][g]
            first[g] = c * ra
            reduced[g] = cols[j + 1][g] - c * slope
            second[g] = reduced[g] * inv
            if g == gj:
                first[g] = jnp.where(sub > sj + 1, first[g], 0.0)
                second[g] = jnp.where(sub > sj + 1, second[g], 0.0)
        for k in range(j + 2, BASE):
            low, high = at(cols[j], k), at(reduced, k)
            for g in range(k // 8, groups):
                cols[k][g] = cols[k][g] - first[g] * low - second[g] * high
        low = at(rows, j)
        high = at(rows, j + 1) - slope * low
        rows[gj] = jnp.where(sub == sj + 1, high, rows[gj])
        for g in range(gj, groups):
            if 8 * g + 7 > j + 1:
                rows[g] = rows[g] - first[g] * low - second[g] * high
    return jnp.concatenate([rows[g] * lax.rsqrt(scales[g]) for g in range(groups)], axis=0)


def factor_block(block, aside):
    rr = lax.broadcasted_iota(jnp.int32, (BLK, BLK), 0)
    cc = lax.broadcasted_iota(jnp.int32, (BLK, BLK), 1)
    diagonal = jnp.where(rr == cc, block, 0.0)
    across = lax.rsqrt(jnp.sum(diagonal, axis=0, keepdims=True))
    down = lax.rsqrt(jnp.sum(diagonal, axis=1, keepdims=True))
    rest = block * across * down
    parts = []
    for p in range(BLK // BASE):
        aside(p)
        done = base_step(p, rest[:BASE])
        parts.append(done)
        if p + 1 < BLK // BASE:
            r1 = (p + 1) * BASE
            lane = lax.broadcasted_iota(jnp.int32, (BLK - r1, BLK), 1)
            update = sdot(left_stack(done)[:, r1:], right_stack(done))
            rest = jnp.where((lane >= r1 - BASE) & (lane < r1), 0.0, rest[BASE:]) - update
    return jnp.where(cc <= rr, jnp.concatenate(parts, axis=0), 0.0) * across


STREAMS = (
    ([(0, j) for j in range(4)], [(0, j) for j in range(4, 8)]),
    ([(1, j) for j in range(1, 5)], [(1, j) for j in range(5, 8)] + [(2, 2)]),
    (
        [(2, j) for j in range(3, 8)] + [(3, j) for j in range(3, 8)],
        [(i, j) for i in range(4, 8) for j in range(i, 8)],
    ),
)
LAST = len(STREAMS) - 1
STREAM_ROWS = [len(stream[0]) * BLK for stream in STREAMS]
STREAM_AT = [sum(STREAM_ROWS[:s]) for s in range(len(STREAMS))]
HALF = sum(STREAM_ROWS)
SIZES = (4, 4, 8)
TILE = 8
WIDE = STREAM_ROWS[LAST] // 8


def packed_blocks():
    return [(s, i, j) for half in range(2) for s in range(len(STREAMS)) for i, j in STREAMS[s][half]]


def runs(pairs):
    found = []
    for i, j in pairs:
        if found and found[-1][0] == i and found[-1][1] + found[-1][2] == j:
            found[-1][2] += 1
        else:
            found.append([i, j, 1])
    return found


def whole_kernel(
    elems, states, scale, nbr, pat, v_hbm, h_hbm, o_ref,
    z_ref, res, mat, left_terms, right_terms, out, send, recv,
    v_ref, h_ref, load, acc, f_ref, y_ref, tail_a, head_a, tail_b, head_b,
    halo_send, halo_recv, swap_send, swap_recv,
    gram, pair, buf_a, buf_b, buf_c, buf_d, buf_e0, buf_e1,
    core_send, core_recv, up_send, up_recv, down_send, down_recv,
):
    count, basis, width = v_ref.shape
    rows = count * basis // states
    per = count // states
    me = lax.axis_index("elem")
    ms = lax.axis_index("state")
    right = lax.rem(me + 1, elems)
    left = lax.rem(me + elems - 1, elems)
    core = lax.rem(me, 2)
    place = [lax.rem(ms, 4), (ms // 4) * 2 + me // 16, lax.rem(me, 16) // 2]

    def device(dim, at, c):
        spot = list(place)
        if dim is not None:
            spot[dim] = at
        x, y, z = spot
        return {"elem": lax.rem(y, 2) * 16 + z * 2 + c, "state": (y // 2) * 4 + x}

    def peer(dim, d):
        return lax.rem(place[dim] + d, SIZES[dim])

    load_v = pltpu.make_async_copy(v_hbm, v_ref, load.at[0])
    load_h = pltpu.make_async_copy(h_hbm, h_ref, load.at[1])
    load_v.start()
    load_h.start()
    greet(
        [{"elem": right}, {"elem": left}]
        + [{"state": lax.rem(ms + d, states)} for d in range(1, states)]
        + [device(1, peer(1, d), core) for d in (1, 3)]
        + [device(2, peer(2, d), core) for d in range(1, 8)]
    )

    halo = ((tail_a, head_a), (tail_b, head_b))

    def exchange(stage, src):
        tail = remote(
            src.at[pl.ds(count - LAYER, LAYER)], halo[stage][0],
            halo_send.at[stage, 0], halo_recv.at[stage, 0], {"elem": right},
        )
        head = remote(
            src.at[pl.ds(0, LAYER)], halo[stage][1],
            halo_send.at[stage, 1], halo_recv.at[stage, 1], {"elem": left},
        )
        return tail, head

    def local_part(src):
        def body(e, carry):
            parts = [src[e]]
            for f in range(6):
                n = nbr[f, e]
                w = (pat[f, e] * (n // count == me).astype(jnp.int32)).astype(F32)
                parts.append(src[lax.rem(n, count)] * jnp.full((basis, width), w, F32).astype(BF16))
            stacked = jnp.concatenate(parts, axis=0)
            acc[e] = jnp.dot(h_ref[e], stacked, preferred_element_type=F32)
            return carry

        lax.fori_loop(0, count, body, 0, unroll=4)

    def image(stage, e, layer):
        face = 0 if layer == 1 else 1
        side = 1 if layer == 1 else 0
        w = pat[face, e].astype(F32)
        block = halo[stage][side][lax.rem(nbr[face, e], LAYER)]
        block = block * jnp.full((basis, width), w, F32).astype(BF16)
        strip = h_ref[e, :, (1 + face) * basis:(2 + face) * basis]
        return acc[e] + jnp.dot(strip, block, preferred_element_type=F32)

    load_v.wait()
    first = exchange(0, v_ref)
    for c in first:
        c.start()
    load_h.wait()
    local_part(v_ref)
    second = exchange(1, f_ref)
    def stage_one(layer):
        first[layer].wait_recv()

        def one(i, carry):
            e = layer * LAYER + i
            f_ref[e] = ((image(0, e, layer) - CENTER * v_ref[e].astype(F32)) / HALF_WIDTH).astype(BF16)
            return carry

        lax.fori_loop(0, LAYER, one, 0, unroll=4)
        second[1 - layer].start()

    for c in range(2):

        @pl.when(core == c)
        def _():
            stage_one(1 - c)
            stage_one(c)

    local_part(f_ref)

    def swap(t, source):
        lanes = pl.ds(pl.multiple_of(source * width, width), width)
        return remote(
            y_ref.at[pl.ds(t * rows, rows)], z_ref.at[:, lanes],
            swap_send.at[t], swap_recv.at[source], {"state": t},
        )

    def stage_two(layer):
        second[layer].wait_recv()

        def two(i, carry):
            e = layer * LAYER + i
            out = 2.0 * (image(1, e, layer) - CENTER * f_ref[e].astype(F32)) / HALF_WIDTH
            y_ref[pl.ds(pl.multiple_of(e * basis, basis), basis), :] = (out - v_ref[e].astype(F32)).astype(BF16)
            return carry

        lax.fori_loop(0, LAYER, two, 0, unroll=4)
        for t in range(layer * states // 2, (layer + 1) * states // 2):

            @pl.when(ms != t)
            def _():
                swap(t, ms).start()

    for c in range(2):

        @pl.when(core == c)
        def _():
            stage_two(1 - c)
            stage_two(c)

    z_ref[:, pl.ds(pl.multiple_of(ms * width, width), width)] = y_ref[
        pl.ds(pl.multiple_of(ms * rows, rows), rows), :
    ]
    for c in first + second:
        c.wait_send()
    for t in range(states):

        @pl.when(ms != t)
        def _():
            swap(t, t).wait_recv()

    other = device(None, None, 1 - core)
    mine = pl.multiple_of(core * HALF, TILE)
    theirs = pl.multiple_of((1 - core) * HALF, TILE)

    def product(half, stream):
        at = half * HALF + STREAM_AT[stream]
        for i, j, n in runs(STREAMS[stream][half]):
            strip = lax.dot_general(
                z_ref[:, i * BLK:(i + 1) * BLK], z_ref[:, j * BLK:(j + n) * BLK],
                (((0,), (0,)), ((), ())), preferred_element_type=F32,
            )
            for b in range(n):
                gram[at:at + BLK, :] = strip[:, b * BLK:(b + 1) * BLK]
                at += BLK

    def hand(stream):
        spot = pl.ds(STREAM_AT[stream], STREAM_ROWS[stream])
        return remote(
            gram.at[pl.ds(theirs + STREAM_AT[stream], STREAM_ROWS[stream])], pair.at[spot],
            core_send.at[stream], core_recv.at[stream], other,
        )

    def both_products(stream):
        for c in range(2):

            @pl.when(core == c)
            def _():
                product(1 - c, stream)
                hand(stream).start()
                product(c, stream)

    buf_e = (buf_e0, buf_e1)
    def ds(start, length):
        return pl.ds(pl.multiple_of(start, TILE), length)

    length_a = [STREAM_ROWS[s] // 8 for s in range(LAST + 1)]
    length_b = [STREAM_ROWS[s] // 32 for s in range(LAST + 1)]
    start_0 = [[mine + STREAM_AT[s] + p * STREAM_ROWS[s] // 2 for p in range(2)] for s in range(LAST + 1)]
    start_a = [[start_0[s][p] + place[p] * length_a[s] for p in range(2)] for s in range(LAST + 1)]
    start_b = [[start_a[s][p] + place[1 - p] * length_b[s] for p in range(2)] for s in range(LAST + 1)]
    started = []

    def launch(copies):
        for c in copies:
            c.start()
        started.extend(copies)
        return copies

    def scatter(level, s):
        length = (length_a, length_b)[level][s]
        copies = []
        for d in range(1, 4):
            for p in range(2):
                dim = p if level == 0 else 1 - p
                to = peer(dim, d)
                start = (start_0, start_a)[level][s][p] + to * length
                copies.append(
                    remote(
                        gram.at[ds(start, length)], (buf_a, buf_b)[level].at[s, p, d, pl.ds(0, length)],
                        up_send.at[level, s, p, d], up_recv.at[level, s, p, d], device(dim, to, core),
                    )
                )
        return launch(copies)

    def gather_sums(level, s, copies):
        length = (length_a, length_b)[level][s]
        for c in copies:
            c.wait_recv()
        for p in range(2):
            own = ds((start_a, start_b)[level][s][p], length)
            total = gram[own, :]
            for d in range(1, 4):
                total = total + (buf_a, buf_b)[level][s, p, d, pl.ds(0, length), :]
            gram[own, :] = total

    def tile_of(z):
        first, second = start_b[LAST]
        return first + (z // 4) * (second - first) + lax.rem(z, 4) * TILE

    def scatter_z(s):
        copies = []
        if s == LAST:
            for d in range(1, 8):
                to = peer(2, d)
                copies.append(
                    remote(
                        gram.at[ds(tile_of(to), TILE)], buf_c.at[d],
                        up_send.at[2, s, 0, d], up_recv.at[2, s, 0, d], device(2, to, core),
                    )
                )
            held, begin_at, length = buf_d, 4 * TILE, TILE
        else:
            held, begin_at, length = buf_e[s], 0, length_b[s]
        for p in range(2):
            held[place[2], p] = gram[ds(start_b[s][p] + begin_at, length), :]
        for d in range(1, 8):
            copies.append(
                remote(
                    held.at[place[2]], held.at[place[2]],
                    up_send.at[2, s, 1, d], up_recv.at[2, s, 1, d], device(2, peer(2, d), core),
                )
            )
        return launch(copies)

    def finish_z(s, copies):
        for c in copies:
            c.wait_recv()
        if s == LAST:
            own = ds(tile_of(place[2]), TILE)
            total = gram[own, :]
            for d in range(1, 8):
                total = total + buf_c[d]
            res[own, :] = total
            held, begin_at, length = buf_d, 4 * TILE, TILE
        else:
            held, begin_at, length = buf_e[s], 0, length_b[s]
        for p in range(2):
            total = held[0, p]
            for z in range(1, 8):
                total = total + held[z, p]
            res[ds(start_b[s][p] + begin_at, length), :] = total

    def spread_z(s):
        own = ds(tile_of(place[2]), TILE)
        return launch([
            remote(
                res.at[own], res.at[own], down_send.at[2, s, 0, d], down_recv.at[2, s, 0, d],
                device(2, peer(2, d), core),
            )
            for d in range(1, 8)
        ])

    def spread(level, s):
        copies = []
        for d in range(1, 4):
            for p in range(2):
                dim = p if level == 0 else 1 - p
                own = ds((start_a, start_b)[level][s][p], (length_a, length_b)[level][s])
                copies.append(
                    remote(
                        res.at[own], res.at[own], down_send.at[level, s, p, d], down_recv.at[level, s, p, d],
                        device(dim, peer(dim, d), core),
                    )
                )
        return launch(copies)

    def arrived(copies):
        for c in copies:
            c.wait_recv()

    def give(s):
        own = ds(mine + STREAM_AT[s], STREAM_ROWS[s])
        return launch([remote(res.at[own], res.at[own], core_send.at[3 + s], core_recv.at[3 + s], other)])

    def with_pair(s):
        hand(s).wait_recv()
        own = ds(mine + STREAM_AT[s], STREAM_ROWS[s])
        gram[own, :] = gram[own, :] + pair[pl.ds(STREAM_AT[s], STREAM_ROWS[s]), :]

    def first_axis(s):
        both_products(s)
        with_pair(s)
        return scatter(0, s)

    def second_axis(s):
        gather_sums(0, s, stage[s])
        return scatter(1, s)

    def along_z(s):
        gather_sums(1, s, stage[s])
        return scatter_z(s)

    def back_along_z(s):
        finish_z(s, stage[s])
        return spread_z(s)

    def back(level, s):
        if level == 1 and s != LAST:
            finish_z(s, stage[s])
        else:
            arrived(stage[s])
        return spread(level, s)

    def back_to_pair(s):
        arrived(stage[s])
        return give(s)

    stage = [None, None, None]
    for s in range(3):
        stage[s] = first_axis(s)
    stage[0] = second_axis(0)
    stage[1] = second_axis(1)
    stage[0] = along_z(0)
    stage[2] = second_axis(2)
    stage[1] = along_z(1)
    stage[2] = along_z(2)
    stage[0] = back(1, 0)
    stage[1] = back(1, 1)
    stage[2] = back_along_z(2)
    stage[0] = back(0, 0)
    stage[1] = back(0, 1)
    stage[2] = back(1, 2)
    stage[0] = back_to_pair(0)
    stage[1] = back_to_pair(1)

    blocks = states * width // BLK
    at = [pl.ds(k * BLK, BLK) for k in range(blocks)]
    own_rows = pl.ds(pl.multiple_of(ms * rows, rows), rows)

    def unpack(stream):
        for spot, (s, i, j) in enumerate(packed_blocks()):
            if s == stream:
                mat[at[i], at[j]] = res[spot * BLK:(spot + 1) * BLK, :] * scale

    def hand_over(t):
        return remote(out.at[t], o_ref.at[own_rows], send.at[t], recv.at[ms], {"state": t})

    def rotate_block(t):
        strip = mat[at[t], :(t + 1) * BLK].astype(BF16)
        out[t] = lax.dot_general(
            z_ref[:, :(t + 1) * BLK], strip, (((1,), (1,)), ((), ())), preferred_element_type=F32
        ).astype(BF16)

    def send_block(t):
        @pl.when(ms == t)
        def _():
            o_ref[own_rows, :] = out[t]

        @pl.when(ms != t)
        def _():
            hand_over(t).start()

    def rest_of_panel(k):
        slot = k % 2
        lhs = left_stack(mat[at[k], at[k]].T)
        places = [pl.ds(0, k * BLK)] if k > 0 else []
        if k + 2 < blocks:
            places.append(pl.ds((k + 2) * BLK, (blocks - k - 2) * BLK))
        for where in places:
            piece = sdot(lhs, right_stack(mat[at[k], where]))
            mat[at[k], where] = piece
            if k + 1 < blocks:
                right_terms[slot, :, where] = right_stack(piece)
        if k + 1 < blocks:
            right_terms[slot, :, at[k]] = right_stack(mat[at[k], at[k]])
        if k + 2 < blocks:
            left_terms[slot, :, where] = left_stack(piece)

    def apply(k, i, diagonal, known=False):
        slot = k % 2
        if diagonal:
            mat[at[i], at[i]] = mat[at[i], at[i]] - sdot(left_terms[slot, :, at[i]], right_terms[slot, :, at[i]])
            return
        lhs = left_terms[slot, :, at[i]]
        old = pl.ds(0, (k + 1) * BLK)
        change = sdot(lhs, right_terms[slot, :, old])
        if k > 0:
            done = pl.ds(0, k * BLK)
            mat[at[i], done] = mat[at[i], done] - change[:, :k * BLK]
        mat[at[i], at[k]] = -change[:, k * BLK:]
        first = i + 1 if known else i
        if first < blocks:
            new = pl.ds(first * BLK, (blocks - first) * BLK)
            mat[at[i], new] = mat[at[i], new] - sdot(lhs, right_terms[slot, :, new])

    for k in range(blocks):
        if k < 3:
            arrived(stage[k])
            unpack(k)
        if k == 1:
            apply(0, 1, True)
        todo = [[(k - 1, i, i == k)] for i in range(k, blocks)]
        if k == 0:
            todo = []
        elif k == 1:
            todo = todo[:1]
        elif k == 2:
            todo = [[(0, i, i == 2), (1, i, i == 2)] for i in range(2, blocks)]

        def aside(p, k=k, todo=todo):
            if p == 0 and k > 0:
                rest_of_panel(k - 1)
                return
            if p == 1 and k > 0:
                rotate_block(k - 1)
            if p == 2 and k == 1:
                apply(0, 2, True)
            if p == 2 and k == 0:
                stage[2] = back(0, 2)
            if p == 3 and k == 1:
                stage[2] = back_to_pair(2)
            for group in todo[max(p - 1, 0)::BLK // BASE - 1]:
                for source, i, known in group:
                    apply(source, i, False, known)

        corner = factor_block(mat[at[k], at[k]], aside)
        mat[at[k], at[k]] = corner
        if k > 0:
            send_block(k - 1)
        if k + 1 < blocks:
            slot = k % 2
            piece = sdot(left_stack(corner.T), right_stack(mat[at[k], at[k + 1]]))
            mat[at[k], at[k + 1]] = piece
            right_terms[slot, :, at[k + 1]] = right_stack(piece)
            left_terms[slot, :, at[k + 1]] = left_stack(piece)
            if k > 0:
                apply(k, k + 1, True)
        else:
            rest_of_panel(k)
            rotate_block(k)
            send_block(k)
    for t in range(states):

        @pl.when(ms != t)
        def _():
            hand_over(t).wait_send()
            rows_of = o_ref.at[pl.ds(t * rows, rows)]
            remote(out.at[t], rows_of, send.at[t], recv.at[t], {"state": t}).wait_recv()
    for c in started:
        c.wait_send()
    for s in range(LAST + 1):
        hand(s).wait_send()
    for t in range(states):

        @pl.when(ms != t)
        def _():
            swap(t, ms).wait_send()


def whole(coefficients, hamiltonian, neighbours, pattern, elems, states):
    count, basis, width = coefficients.shape
    rows = count * basis // states
    n = states * width
    scale = 1.0 / (count * elems * basis)
    dma = pltpu.SemaphoreType.DMA
    return pl.pallas_call(
        functools.partial(whole_kernel, elems, states, scale),
        out_shape=jax.ShapeDtypeStruct((count * basis, width), BF16),
        in_specs=[in_smem(), in_smem(), in_hbm(), in_hbm()],
        out_specs=in_vmem(),
        scratch_shapes=[
            VMEM((rows, n), BF16),
            VMEM((2 * HALF, BLK), F32),
            VMEM((n, n), F32),
            VMEM((2, 6 * BLK, n), BF16),
            VMEM((2, 6 * BLK, n), BF16),
            VMEM((states, rows, width), BF16),
            dma((states,)),
            dma((states,)),
            VMEM(coefficients.shape, BF16),
            VMEM(hamiltonian.shape, BF16),
            dma((2,)),
            VMEM((count, basis, width), F32),
            VMEM((count, basis, width), BF16),
            VMEM((count * basis, width), BF16),
            VMEM((LAYER, basis, width), BF16),
            VMEM((LAYER, basis, width), BF16),
            VMEM((LAYER, basis, width), BF16),
            VMEM((LAYER, basis, width), BF16),
            dma((2, 2)),
            dma((2, 2)),
            dma((states,)),
            dma((states,)),
            VMEM((2 * HALF, BLK), F32),
            VMEM((HALF, BLK), F32),
            VMEM((3, 2, 4, WIDE, BLK), F32),
            VMEM((3, 2, 4, WIDE // 4, BLK), F32),
            VMEM((8, TILE, BLK), F32),
            VMEM((8, 2, TILE, BLK), F32),
            VMEM((8, 2, STREAM_ROWS[0] // 32, BLK), F32),
            VMEM((8, 2, STREAM_ROWS[1] // 32, BLK), F32),
            dma((6,)),
            dma((6,)),
            dma((3, 3, 2, 8)),
            dma((3, 3, 2, 8)),
            dma((3, 3, 2, 8)),
            dma((3, 3, 2, 8)),
        ],
        compiler_params=pltpu.CompilerParams(
            collective_id=0, has_side_effects=True, vmem_limit_bytes=60 * MIB
        ),
        cost_estimate=pl.CostEstimate(flops=12 * 10**9, bytes_accessed=8 * MIB, transcendentals=0),
    )(neighbours.T, pattern.T, coefficients, hamiltonian)


def on_device(coefficients, hamiltonian, neighbours, pattern):
    count, basis, width = coefficients.shape
    elems = lax.axis_size("elem")
    states = lax.axis_size("state")
    result = whole(coefficients, hamiltonian, neighbours, pattern, elems, states)
    return result.reshape(count, basis, width)


def solution(mesh):
    return jax.shard_map(
        on_device,
        mesh=mesh,
        in_specs=(
            P("elem", None, "state"),
            P("elem", None, None),
            P("elem", None),
            P("elem", None),
        ),
        out_specs=P("elem", None, "state"),
        check_vma=False,
    )
```
